256 devices in a mesh: seq: 32 (over y, z), head: 8 (over x, core).
Axes of the slice: x: 4, y: 4, z: 8, core: 2. Of those that a mesh axis runs over, the one named last changes fastest.
Arguments:
- query: bfloat16 [16384, 8192], P('seq', 'head'), may hold values from -1.5 to 1.5
- key_in: bfloat16 [16384, 8192], P('seq', 'head'), may hold values from -0.5 to 0.5
- value: bfloat16 [16384, 8192], P('seq', 'head'), may hold values from -6 to 6
- gate: bfloat16 [16384, 8192], P(('seq', 'head')), may hold values from -6 to 6
- gain: float32 [8192], replicated, may hold values from 0.5 to 1.5
- grad_out: bfloat16 [16384, 8192], P(('seq', 'head')), may hold values from -6 to 6
Outputs:
- grad_query: bfloat16 [16384, 8192], P('seq', 'head')
- grad_key: bfloat16 [16384, 8192], P('seq', 'head')
- grad_value: bfloat16 [16384, 8192], P('seq', 'head')
- grad_gate: bfloat16 [16384, 8192], P(('seq', 'head'))
The draws below stay inside these ranges and needn't reach their ends.
All inputs are finite; a program needn't handle non-finite values.
Results may differ from the reference program's by a relative error of at most 0.012.
Values may be sent and summed in bfloat16 or wider, within the bound.
No kernel may reach another device: no remote copies, remote signals or barrier semaphores. Data moves between devices by JAX's collectives and lax.ppermute only.
A program may use at most 128 MiB of HBM per device.

```python
import jax
import jax.numpy as jnp
from jax import lax

HEADS = 64
HEAD_DIM = 128
TOK_DEV = 512
TOKENS = 16384
WIDTH = 8192
N_SEQ = 32


def block_scale(key, dims, shards, least, high):
    level = 1.0
    for dim, shards_of in shards:
        heights = jax.random.uniform(jax.random.fold_in(jax.random.fold_in(key, 6), dim), (shards_of,), jnp.float32, least / len(shards), high / len(shards))
        level = level * jnp.repeat(jnp.exp(heights), dims[dim] // shards_of).reshape((-1,) + (1,) * (len(dims) - 1 - dim))
    return level


def centred(own_key, shape, deviation, most, split=(), kind=jnp.bfloat16):
    level = block_scale(own_key, shape, split, -0.22, 0.18) if split else 1.0
    entries = jax.random.normal(own_key, shape, jnp.float32) * deviation * level
    return jnp.minimum(jnp.maximum(entries, -most), most).astype(kind)


def setup_inputs(seed: int = 0) -> dict:
    seeds = jax.random.split(jax.random.key(seed), 7)
    return {
        "query": centred(seeds[0], (TOKENS, WIDTH), 0.25, 1.5, ((0, 32), (1, 8))),
        "key_in": centred(seeds[1], (TOKENS, WIDTH), HEAD_DIM ** -0.5, 0.5, ((0, 32), (1, 8))),
        "value": centred(seeds[2], (TOKENS, WIDTH), 1.0, 6.0, ((0, 32), (1, 8))),
        "gate": centred(seeds[3], (TOKENS, WIDTH), 1.0, 6.0, ((0, 256),)),
        "gain": jnp.clip(1.0 + 0.1 * jax.random.normal(seeds[4], (WIDTH,), jnp.float32), 0.5, 1.5),
        "grad_out": centred(seeds[5], (TOKENS, WIDTH), 1.0, 6.0, ((0, 256),)),
    }


def reference(query, key_in, value, gate, gain, grad_out):
    blocks = N_SEQ
    tok_block = TOK_DEV
    width_all = HEADS * HEAD_DIM
    queries = query.reshape(blocks, tok_block, HEADS, HEAD_DIM)
    keys_all = key_in.reshape(blocks, tok_block, HEADS, HEAD_DIM)
    values_all = value.reshape(blocks, tok_block, HEADS, HEAD_DIM)
    block_state = jnp.einsum('bthd,bthe->bhde', keys_all.astype(jnp.float32), values_all.astype(jnp.float32))
    zero_state = jnp.zeros((1, HEADS, HEAD_DIM, HEAD_DIM), jnp.float32)
    prefix = jnp.concatenate([zero_state, jnp.cumsum(block_state[:-1], axis=0)], axis=0)
    causal = jnp.tril(jnp.ones((tok_block, tok_block), dtype=bool))

    def forward_block(operands):
        q_block, k_block, v_block, p_block = operands
        scores = jnp.einsum('thd,shd->hts', q_block.astype(jnp.float32), k_block.astype(jnp.float32))
        masked_scores = jnp.where(causal[None], scores, 0.0).astype(jnp.bfloat16)
        prefix_low = p_block.astype(jnp.bfloat16)
        result = jnp.einsum('hts,she->the', masked_scores.astype(jnp.float32), v_block.astype(jnp.float32))
        result = result + jnp.einsum('thd,hde->the', q_block.astype(jnp.float32), prefix_low.astype(jnp.float32))
        return result.astype(jnp.bfloat16)
    attn_out = lax.map(forward_block, (queries, keys_all, values_all, prefix))
    attn_out = attn_out.reshape(blocks, tok_block, width_all)
    gate_blocks = gate.reshape(blocks, tok_block, width_all)
    grad_blocks = grad_out.reshape(blocks, tok_block, width_all)

    def norm_block(operands):
        out_block, gate_block, grad_block = operands
        rows_wide = out_block.astype(jnp.float32)
        inv_rms = lax.rsqrt(lax.optimization_barrier(jnp.mean(rows_wide * rows_wide, axis=1, keepdims=True)) + 1e-06)
        normed = rows_wide * inv_rms
        gate_wide = gate_block.astype(jnp.float32)
        sigmoid_gate = jax.nn.sigmoid(gate_wide)
        scaled = grad_block.astype(jnp.float32) * gain[None, :]
        grad_gate = (scaled * normed * sigmoid_gate * (1.0 + gate_wide * (1.0 - sigmoid_gate))).astype(jnp.bfloat16)
        weighted = scaled * gate_wide * sigmoid_gate
        grad_attn = inv_rms * (weighted - normed * lax.optimization_barrier(jnp.mean(weighted * normed, axis=1, keepdims=True)))
        return (grad_attn.astype(jnp.bfloat16), grad_gate)
    grad_attn, grad_gate = lax.map(norm_block, (attn_out, gate_blocks, grad_blocks))
    grad_attn = grad_attn.reshape(blocks, tok_block, HEADS, HEAD_DIM)
    block_grad = jnp.einsum('bthd,bthe->bhde', queries.astype(jnp.float32), grad_attn.astype(jnp.float32))
    flipped = jnp.flip(block_grad, axis=0)
    suffix = jnp.flip(jnp.concatenate([zero_state, jnp.cumsum(flipped[:-1], axis=0)], axis=0), axis=0)

    def backward_block(operands):
        q_block, k_block, v_block, do_block, p_block, s_block = operands
        q_wide = q_block.astype(jnp.float32)
        k_wide = k_block.astype(jnp.float32)
        v_wide = v_block.astype(jnp.float32)
        do_wide = do_block.astype(jnp.float32)
        prefix_low = p_block.astype(jnp.bfloat16).astype(jnp.float32)
        suffix_low = s_block.astype(jnp.bfloat16).astype(jnp.float32)
        scores = jnp.einsum('thd,shd->hts', q_wide, k_wide)
        masked_scores = jnp.where(causal[None], scores, 0.0).astype(jnp.bfloat16).astype(jnp.float32)
        grad_scores = jnp.where(causal[None], jnp.einsum('the,she->hts', do_wide, v_wide), 0.0)
        grad_scores = grad_scores.astype(jnp.bfloat16).astype(jnp.float32)
        grad_query = jnp.einsum('hts,shd->thd', grad_scores, k_wide) + jnp.einsum('the,hde->thd', do_wide, prefix_low)
        grad_key = jnp.einsum('hts,thd->shd', grad_scores, q_wide) + jnp.einsum('she,hde->shd', v_wide, suffix_low)
        grad_value = jnp.einsum('hts,the->she', masked_scores, do_wide) + jnp.einsum('shd,hde->she', k_wide, suffix_low)
        return (grad_query.astype(jnp.bfloat16), grad_key.astype(jnp.bfloat16), grad_value.astype(jnp.bfloat16))
    grad_query, grad_key, grad_value = lax.map(backward_block, (queries, keys_all, values_all, grad_attn, prefix, suffix))
    total_rows = blocks * tok_block
    return (grad_query.reshape(total_rows, width_all), grad_key.reshape(total_rows, width_all), grad_value.reshape(total_rows, width_all), grad_gate.reshape(total_rows, width_all))
```

```python
import functools

import jax
import jax.numpy as jnp
from jax import lax
from jax.experimental import pallas as pl
from jax.experimental.pallas import tpu as pltpu
from jax.sharding import PartitionSpec as P

HEAD_DIM = 128
EPS = 1e-06
F32 = jnp.float32
BF16 = jnp.bfloat16


def mm(a, b):
    return lax.dot_general(a, b, (((1,), (0,)), ((), ())), preferred_element_type=F32)


def mm_bt(a, b):
    return lax.dot_general(a, b, (((1,), (1,)), ((), ())), preferred_element_type=F32)


def mm_at(a, b):
    return lax.dot_general(a, b, (((0,), (0,)), ((), ())), preferred_element_type=F32)


def call(kernel, out_shape, grid, in_specs, out_specs, flops, nbytes, name):
    specs = dict(grid=grid, in_specs=in_specs, out_specs=out_specs) if grid else {}
    return pl.pallas_call(
        kernel,
        out_shape=out_shape,
        **specs,
        compiler_params=pltpu.CompilerParams(vmem_limit_bytes=24 * 2**20),
        cost_estimate=pl.CostEstimate(flops=flops, bytes_accessed=nbytes, transcendentals=0),
        name=name,
    )


def state_kernel(a_ref, b_ref, s_ref):
    both = mm_at(a_ref[...], b_ref[...])
    d = HEAD_DIM
    for h in range(2):
        s_ref[h] = both[h * d : (h + 1) * d, h * d : (h + 1) * d].astype(s_ref.dtype)


def running_kernel(reverse, x_ref, o_ref):
    n = x_ref.shape[0]
    total = jnp.zeros(x_ref.shape[1:], F32)
    for k in range(n):
        at = n - 1 - k if reverse else k
        o_ref[at] = total.astype(o_ref.dtype)
        total = total + x_ref[at].astype(F32)


def weigh_kernel(gate_ref, grad_ref, gain_ref, w_ref):
    g = gate_ref[...].astype(F32)
    w = grad_ref[...].astype(F32) * gain_ref[...] * g * jax.nn.sigmoid(g)
    w_ref[0] = w.astype(w_ref.dtype)


def lower(n):
    return lax.broadcasted_iota(jnp.int32, (n, n), 0) >= lax.broadcasted_iota(jnp.int32, (n, n), 1)


def upper(n):
    return lax.broadcasted_iota(jnp.int32, (n, n), 0) <= lax.broadcasted_iota(jnp.int32, (n, n), 1)


def intra_kernel(q_ref, k_ref, v_ref, i_ref):
    d = HEAD_DIM
    t = q_ref.shape[0]
    half = t // 2
    keep = lower(half)
    for h in range(2):
        cols = slice(h * d, (h + 1) * d)
        q, k, v = q_ref[:, cols], k_ref[:, cols], v_ref[:, cols]
        for r in range(2):
            rows = slice(r * half, (r + 1) * half)
            s = mm_bt(q[rows], k[rows])
            s = jnp.where(keep, s, 0.0).astype(BF16)
            acc = mm(s, v[rows])
            if r:
                s = mm_bt(q[rows], k[:half]).astype(BF16)
                acc = acc + mm(s, v[:half])
            i_ref[rows, cols] = acc


def out_kernel(i_ref, q_ref, p_ref, w_ref, o_ref, sums_ref, sq_ref, cross_ref):
    d = HEAD_DIM
    step = pl.program_id(0)
    sq, cross = None, None
    for h in range(2):
        cols = slice(h * d, (h + 1) * d)
        o = (i_ref[:, cols] + mm(q_ref[:, cols], p_ref[h])).astype(BF16)
        o_ref[:, cols] = o
        o = o.astype(F32)
        a, b = o * o, o * w_ref[:, cols].astype(F32)
        sq, cross = (a, b) if sq is None else (sq + a, cross + b)

    @pl.when(step == 0)
    def _():
        sq_ref[...] = sq
        cross_ref[...] = cross

    @pl.when(step > 0)
    def _():
        sq_ref[...] += sq
        cross_ref[...] += cross

    @pl.when(step == pl.num_programs(0) - 1)
    def _():
        blocks = sq_ref.shape[0] // 128
        rows = []
        for ref in (sq_ref, cross_ref):
            for r in range(blocks):
                piece = jnp.transpose(ref[r * 128 : (r + 1) * 128, :])
                rows.append(jnp.sum(piece, axis=0, keepdims=True))
        tile = jnp.concatenate(rows, axis=0)
        for k in range(sums_ref.shape[0]):
            sums_ref[k] = tile


def grad_kernel(width, sums_ref, w_ref, o_ref, q_ref, do_ref, z_ref):
    d = HEAD_DIM
    tile = jnp.sum(sums_ref[...], axis=0)
    turned = jnp.transpose(jnp.broadcast_to(tile[None], (16,) + tile.shape).reshape(128, 128))
    blocks = tile.shape[0] // 2
    inv = lax.rsqrt(turned[:, :blocks] / width + EPS)
    fall = inv * inv * inv * (turned[:, blocks : 2 * blocks] / width)
    inv = jnp.concatenate([inv[:, r : r + 1] for r in range(blocks)], axis=0)
    fall = jnp.concatenate([fall[:, r : r + 1] for r in range(blocks)], axis=0)
    do = (inv * w_ref[...].astype(F32) - fall * o_ref[...].astype(F32)).astype(BF16)
    do_ref[...] = do
    both = mm_at(q_ref[...], do)
    for h in range(2):
        z_ref[h] = both[h * d : (h + 1) * d, h * d : (h + 1) * d].astype(z_ref.dtype)


def back_kernel(q_ref, k_ref, v_ref, do_ref, p_ref, gq_ref, gk_ref, gv_ref):
    d = HEAD_DIM
    t = q_ref.shape[0]
    half = t // 2
    low, up = lower(half), upper(half)
    one, two = slice(0, half), slice(half, t)
    for h in range(2):
        cols = slice(h * d, (h + 1) * d)
        q, k, v, do = q_ref[:, cols], k_ref[:, cols], v_ref[:, cols], do_ref[:, cols]
        for r in (one, two):
            g = jnp.where(low, mm_bt(do[r], v[r]), 0.0).astype(BF16)
            acc = mm(g, k[r]) + mm_bt(do[r], p_ref[h])
            if r is two:
                acc = acc + mm(mm_bt(do[r], v[one]).astype(BF16), k[one])
            gq_ref[r, cols] = acc.astype(BF16)
            gt = jnp.where(up, mm_bt(v[r], do[r]), 0.0).astype(BF16)
            st = jnp.where(up, mm_bt(k[r], q[r]), 0.0).astype(BF16)
            ak, av = mm(gt, q[r]), mm(st, do[r])
            if r is one:
                ak = ak + mm(mm_bt(v[r], do[two]).astype(BF16), q[two])
                av = av + mm(mm_bt(k[r], q[two]).astype(BF16), do[two])
            gk_ref[r, cols] = ak
            gv_ref[r, cols] = av


def last_kernel(ak_ref, av_ref, k_ref, v_ref, s_ref, gk_ref, gv_ref):
    d = HEAD_DIM
    for h in range(2):
        cols = slice(h * d, (h + 1) * d)
        gk_ref[:, cols] = (ak_ref[:, cols] + mm_bt(v_ref[:, cols], s_ref[h])).astype(BF16)
        gv_ref[:, cols] = (av_ref[:, cols] + mm(k_ref[:, cols], s_ref[h])).astype(BF16)


def gate_kernel(rows_ref, gate_ref, grad_ref, gain_ref, gg_ref):
    parts, _, wide = rows_ref.shape
    total = None
    for p in range(parts):
        o = rows_ref[p].astype(F32)
        s = jnp.sum(o * o, axis=1, keepdims=True)
        total = s if total is None else total + s
    inv = lax.rsqrt(total / (parts * wide) + EPS)
    for p in range(parts):
        cols = slice(p * wide, (p + 1) * wide)
        g = gate_ref[:, cols].astype(F32)
        s = jax.nn.sigmoid(g)
        scaled = grad_ref[:, cols].astype(F32) * gain_ref[:, cols]
        normed = rows_ref[p].astype(F32) * inv
        gg_ref[:, cols] = (scaled * normed * s * (1.0 + g * (1.0 - s))).astype(BF16)


def on_device(query, key_in, value, gate, gain, grad_out):
    d = HEAD_DIM
    t, own = query.shape
    heads = own // d
    rows, width = gate.shape
    n_seq, n_head = lax.axis_size("seq"), lax.axis_size("head")
    pairs = heads // 2
    gain = gain.reshape(1, width)

    def sds(shape, dtype):
        return jax.ShapeDtypeStruct(shape, dtype)

    wide = pl.BlockSpec((t, 2 * d), lambda i: (0, i))
    square = pl.BlockSpec((2, d, d), lambda i: (i, 0, 0))
    small = 2 * t * d * d * heads
    large = 2 * t * t * d * heads

    def exchange(states, reverse):
        piece = (n_seq, heads * d // n_seq, d)
        states = lax.all_to_all(states.reshape(piece), "seq", 0, 0, tiled=True)
        summed = call(
            functools.partial(running_kernel, reverse), sds(piece, BF16), (), None, None,
            heads * d * d, 4 * heads * d * d, "running",
        )(states)
        return lax.all_to_all(summed, "seq", 0, 0, tiled=True).reshape(heads, d, d)

    states = call(
        state_kernel, sds((heads, d, d), BF16), (pairs,), [wide, wide], square,
        2 * small, 4 * t * own, "states",
    )(key_in, value)
    prefix = exchange(states, False)

    part = pl.BlockSpec((rows, own), lambda i: (0, i))
    weighted = call(
        weigh_kernel, sds((n_head, rows, own), BF16), (n_head,),
        [part, part, pl.BlockSpec((1, own), lambda i: (0, i))],
        pl.BlockSpec((1, rows, own), lambda i: (i, 0, 0)),
        20 * rows * width, 6 * rows * width, "weigh",
    )(gate, grad_out, gain)
    weighted = lax.all_to_all(weighted, "head", 0, 0, tiled=True).reshape(t, own)

    intra = call(
        intra_kernel, sds((t, own), F32), (pairs,), [wide, wide, wide], wide,
        2 * large, 10 * t * own, "intra",
    )(query, key_in, value)

    tile = (n_head, 2 * t // 128, 128)
    out, sums = pl.pallas_call(
        out_kernel,
        out_shape=(sds((t, own), BF16), sds(tile, F32)),
        grid=(pairs,),
        in_specs=[wide, wide, square, wide],
        out_specs=(wide, pl.BlockSpec(tile, lambda i: (0, 0, 0))),
        scratch_shapes=[pltpu.VMEM((t, d), F32), pltpu.VMEM((t, d), F32)],
        compiler_params=pltpu.CompilerParams(vmem_limit_bytes=24 * 2**20),
        cost_estimate=pl.CostEstimate(flops=small, bytes_accessed=10 * t * own, transcendentals=0),
        name="outs",
    )(intra, query, prefix, weighted)
    sums = lax.all_to_all(sums, "head", 0, 0, tiled=True)

    grad_attn, states = call(
        functools.partial(grad_kernel, float(width)),
        (sds((t, own), BF16), sds((heads, d, d), BF16)), (pairs,),
        [pl.BlockSpec(tile, lambda i: (0, 0, 0)), wide, wide, wide], (wide, square),
        small, 8 * t * own, "grads",
    )(sums, weighted, out, query)
    suffix = exchange(states, True)

    token_rows = lax.all_to_all(out.reshape(n_head, rows, own), "head", 0, 0, tiled=True)
    grad_gate = call(
        gate_kernel, sds((rows, width), BF16), (), None, None,
        20 * rows * width, 8 * rows * width, "gates",
    )(token_rows, gate, grad_out, gain)

    grad_query, part_key, part_value = call(
        back_kernel,
        (sds((t, own), BF16), sds((t, own), F32), sds((t, own), F32)), (pairs,),
        [wide, wide, wide, wide, square], (wide, wide, wide),
        4 * large, 18 * t * own, "backs",
    )(query, key_in, value, grad_attn, prefix)

    grad_key, grad_value = call(
        last_kernel, (sds((t, own), BF16), sds((t, own), BF16)), (pairs,),
        [wide, wide, wide, wide, square], (wide, wide),
        2 * small, 16 * t * own, "last",
    )(part_key, part_value, key_in, value, suffix)
    return grad_query, grad_key, grad_value, grad_gate


def solution(mesh):
    in_specs = (
        P("seq", "head"),
        P("seq", "head"),
        P("seq", "head"),
        P(("seq", "head"), None),
        P(),
        P(("seq", "head"), None),
    )
    out_specs = (P("seq", "head"), P("seq", "head"), P("seq", "head"), P(("seq", "head"), None))
    return jax.shard_map(
        on_device, mesh=mesh, in_specs=in_specs, out_specs=out_specs, check_vma=False
    )
```

```python
import functools

import jax
import jax.numpy as jnp
from jax import lax
from jax.experimental import pallas as pl
from jax.experimental.pallas import tpu as pltpu
from jax.sharding import PartitionSpec as P

HEAD_DIM = 128
EPS = 1e-06
F32 = jnp.float32
BF16 = jnp.bfloat16


def mm(a, b):
    return lax.dot_general(a, b, (((1,), (0,)), ((), ())), preferred_element_type=F32)


def mm_bt(a, b):
    return lax.dot_general(a, b, (((1,), (1,)), ((), ())), preferred_element_type=F32)


def mm_at(a, b):
    return lax.dot_general(a, b, (((0,), (0,)), ((), ())), preferred_element_type=F32)


def params():
    return pltpu.CompilerParams(vmem_limit_bytes=24 * 2**20)


def cost(flops, nbytes):
    return pl.CostEstimate(flops=int(flops), bytes_accessed=int(nbytes), transcendentals=0)


def in_hbm(x):
    return pltpu.with_memory_space_constraint(x, pltpu.HBM)


def partner(n, d, sign):
    me = lax.axis_index("head")
    chip, core = me // 2, me % 2
    flip = core + d % 2 - 2 * core * (d % 2)
    return lax.rem(chip + sign * (d // 2) + n // 2, n // 2) * 2 + flip


def send_all(pieces):
    n = len(pieces)
    got = [pieces[0]]
    for d in range(1, n):
        pairs = [(i, ((i // 2 + d // 2) % (n // 2)) * 2 + ((i % 2) ^ (d % 2))) for i in range(n)]
        got.append(lax.ppermute(pieces[d], "head", pairs))
    return got


def start_all(copies):
    for c in copies:
        c.start()
    return copies


def wait_all(copies):
    for c in copies:
        c.wait()


def columns(i):
    return pl.ds(2 * HEAD_DIM * i, 2 * HEAD_DIM)


def by_pairs(src, dst, sems, at):
    n = src.shape[1] // (2 * HEAD_DIM)
    return [
        pltpu.make_async_copy(src.at[:, columns(i)], dst.at[:, columns(i)], sems.at[at + i])
        for i in range(n)
    ]


def rows_of(n, d, sign, rows):
    return pl.ds(pl.multiple_of(partner(n, d, sign) * rows, rows), rows)


def assemble(pieces, dst, sems, at):
    n, rows = len(pieces), pieces[0].shape[0]
    return [
        pltpu.make_async_copy(pieces[d], dst.at[rows_of(n, d, -1, rows), :], sems.at[at + d])
        for d in range(n)
    ]


def state_kernel(a_hbm, b_hbm, s_ref, a_ref, b_ref, sems):
    d = HEAD_DIM
    n = s_ref.shape[0] // 2
    ca, cb = by_pairs(a_hbm, a_ref, sems, 0), by_pairs(b_hbm, b_ref, sems, n)
    for i in range(n):
        ca[i].start()
        cb[i].start()
    for i in range(n):
        ca[i].wait()
        cb[i].wait()
        both = mm_at(a_ref[:, columns(i)], b_ref[:, columns(i)])
        for h in range(2):
            s_ref[2 * i + h] = both[h * d : (h + 1) * d, h * d : (h + 1) * d].astype(s_ref.dtype)


def running_kernel(reverse, x_ref, o_ref):
    n = x_ref.shape[0]
    total = jnp.zeros(x_ref.shape[1:], F32)
    for k in range(n):
        at = n - 1 - k if reverse else k
        o_ref[at] = total.astype(o_ref.dtype)
        total = total + x_ref[at].astype(F32)


def weigh_kernel(gate_ref, grad_ref, gain_ref, *w_refs):
    n = len(w_refs)
    own = gate_ref.shape[1] // n
    for d in range(n):
        cols = pl.ds(pl.multiple_of(partner(n, d, 1) * own, own), own)
        g = gate_ref[:, cols].astype(F32)
        w = grad_ref[:, cols].astype(F32) * gain_ref[:, cols] * g * jax.nn.sigmoid(g)
        w_refs[d][...] = w.astype(BF16)


def lower(n):
    return lax.broadcasted_iota(jnp.int32, (n, n), 0) >= lax.broadcasted_iota(jnp.int32, (n, n), 1)


def upper(n):
    return lax.broadcasted_iota(jnp.int32, (n, n), 0) <= lax.broadcasted_iota(jnp.int32, (n, n), 1)


def intra_kernel(q_ref, k_ref, v_ref, i_ref):
    d = HEAD_DIM
    t = q_ref.shape[0]
    half = t // 2
    keep = lower(half)
    for h in range(2):
        cols = slice(h * d, (h + 1) * d)
        q, k, v = q_ref[:, cols], k_ref[:, cols], v_ref[:, cols]
        for r in range(2):
            rows = slice(r * half, (r + 1) * half)
            s = mm_bt(q[rows], k[rows])
            s = jnp.where(keep, s, 0.0).astype(BF16)
            acc = mm(s, v[rows])
            if r:
                s = mm_bt(q[rows], k[:half]).astype(BF16)
                acc = acc + mm(s, v[:half])
            i_ref[rows, cols] = acc


def out_kernel(n_head, *refs):
    i_hbm, q_hbm, p_ref = refs[:3]
    w_hbm = refs[3 : 3 + n_head]
    sums_ref = refs[3 + n_head]
    o_hbm = refs[4 + n_head : 4 + 2 * n_head]
    i_ref, q_ref, w_ref, o_ref, sq_ref, cross_ref, sems, out_sems = refs[4 + 2 * n_head :]
    d = HEAD_DIM
    t, own = q_ref.shape
    n = own // (2 * d)
    ci, cq = by_pairs(i_hbm, i_ref, sems, 0), by_pairs(q_hbm, q_ref, sems, n)
    for i in range(n):
        cq[i].start()
        ci[i].start()
    cw = start_all(assemble(w_hbm, w_ref, sems, 2 * n))
    for i in range(n):
        cq[i].wait()
        ci[i].wait()
        for h in range(2 * i, 2 * i + 2):
            cols = slice(h * d, (h + 1) * d)
            for r in range(0, t, 256):
                rows = slice(r, r + 256)
                o = i_ref[rows, cols] + mm(q_ref[rows, cols], p_ref[h])
                o_ref[rows, cols] = o.astype(BF16)
    rows = t // n_head
    co = start_all(
        [
            pltpu.make_async_copy(o_ref.at[rows_of(n_head, k, 1, rows), :], o_hbm[k], out_sems.at[k])
            for k in range(n_head)
        ]
    )
    wait_all(cw)
    blocks = t // d
    lines = [None] * (2 * blocks)
    for r in range(blocks):
        rows = slice(r * d, (r + 1) * d)
        sq, cross = None, None
        for h in range(2 * n):
            cols = slice(h * d, (h + 1) * d)
            o = o_ref[rows, cols].astype(F32)
            a, b = o * o, o * w_ref[rows, cols].astype(F32)
            sq, cross = (a, b) if sq is None else (sq + a, cross + b)
        lines[r] = jnp.sum(jnp.transpose(sq), axis=0, keepdims=True)
        lines[blocks + r] = jnp.sum(jnp.transpose(cross), axis=0, keepdims=True)
    tile = jnp.concatenate(lines, axis=0)
    for k in range(n_head):
        sums_ref[k] = tile
    wait_all(co)


def grad_kernel(n_head, width, *refs):
    sums_ref, q_hbm = refs[:2]
    w_hbm = refs[2 : 2 + n_head]
    o_hbm = refs[2 + n_head : 2 + 2 * n_head]
    z_ref, do_hbm, q_ref, w_ref, o_ref, do_ref, sems, out_sems = refs[2 + 2 * n_head :]
    d = HEAD_DIM
    t, own = q_ref.shape
    n = own // (2 * d)
    rows = t // n_head
    cw = start_all(assemble(w_hbm, w_ref, sems, 0))
    co = start_all(
        [
            pltpu.make_async_copy(
                o_hbm[k], o_ref.at[rows_of(n_head, k, 1, rows), :], sems.at[n_head + k]
            )
            for k in range(n_head)
        ]
    )
    cq = start_all(by_pairs(q_hbm, q_ref, sems, 2 * n_head))
    tile = jnp.sum(sums_ref[...], axis=0)
    blocks = t // d
    turned = jnp.transpose(jnp.concatenate([tile] * (d // tile.shape[0]), axis=0))
    inv = lax.rsqrt(turned[:, :blocks] / width + EPS)
    fall = inv * inv * inv * (turned[:, blocks : 2 * blocks] / width)
    inv = [jnp.broadcast_to(inv[:, r : r + 1], (d, d)) for r in range(blocks)]
    fall = [jnp.broadcast_to(fall[:, r : r + 1], (d, d)) for r in range(blocks)]
    wait_all(cw)
    wait_all(co)
    cd = by_pairs(do_ref, do_hbm, out_sems, 0)
    for i in range(n):
        for h in range(2 * i, 2 * i + 2):
            cols = slice(h * d, (h + 1) * d)
            for r in range(blocks):
                rows = slice(r * d, (r + 1) * d)
                w, o = w_ref[rows, cols].astype(F32), o_ref[rows, cols].astype(F32)
                do_ref[rows, cols] = (inv[r] * w - fall[r] * o).astype(BF16)
        cd[i].start()
        cq[i].wait()
        both = mm_at(q_ref[:, columns(i)], do_ref[:, columns(i)])
        for h in range(2):
            z_ref[2 * i + h] = both[h * d : (h + 1) * d, h * d : (h + 1) * d].astype(z_ref.dtype)
    wait_all(cd)


def back_kernel(q_ref, k_ref, v_ref, do_ref, p_ref, gq_ref, gk_ref, gv_ref):
    d = HEAD_DIM
    t = q_ref.shape[0]
    half = t // 2
    low, up = lower(half), upper(half)
    one, two = slice(0, half), slice(half, t)
    for h in range(2):
        cols = slice(h * d, (h + 1) * d)
        q, k, v, do = q_ref[:, cols], k_ref[:, cols], v_ref[:, cols], do_ref[:, cols]
        for r in (one, two):
            g = jnp.where(low, mm_bt(do[r], v[r]), 0.0).astype(BF16)
            acc = mm(g, k[r]) + mm_bt(do[r], p_ref[h])
            if r is two:
                acc = acc + mm(mm_bt(do[r], v[one]).astype(BF16), k[one])
            gq_ref[r, cols] = acc.astype(BF16)
            gt = jnp.where(up, mm_bt(v[r], do[r]), 0.0).astype(BF16)
            st = jnp.where(up, mm_bt(k[r], q[r]), 0.0).astype(BF16)
            ak, av = mm(gt, q[r]), mm(st, do[r])
            if r is one:
                ak = ak + mm(mm_bt(v[r], do[two]).astype(BF16), q[two])
                av = av + mm(mm_bt(k[r], q[two]).astype(BF16), do[two])
            gk_ref[r, cols] = ak
            gv_ref[r, cols] = av


def last_kernel(ak_hbm, av_hbm, k_hbm, v_hbm, s_ref, gk_hbm, gv_hbm, ak_ref, av_ref, k_ref, v_ref, gk_ref, gv_ref, sems, out_sems):
    d = HEAD_DIM
    t, own = k_ref.shape
    n = own // (2 * d)
    ins = [
        by_pairs(src, dst, sems, n * k)
        for k, (src, dst) in enumerate(
            ((v_hbm, v_ref), (ak_hbm, ak_ref), (k_hbm, k_ref), (av_hbm, av_ref))
        )
    ]
    for i in range(n):
        for c in ins:
            c[i].start()
    ck, cv = by_pairs(gk_ref, gk_hbm, out_sems, 0), by_pairs(gv_ref, gv_hbm, out_sems, n)
    for i in range(n):
        for c in ins:
            c[i].wait()
        for h in range(2 * i, 2 * i + 2):
            cols = slice(h * d, (h + 1) * d)
            for r in range(0, t, 256):
                rows = slice(r, r + 256)
                gk = ak_ref[rows, cols] + mm_bt(v_ref[rows, cols], s_ref[h])
                gk_ref[rows, cols] = gk.astype(BF16)
                gv = av_ref[rows, cols] + mm(k_ref[rows, cols], s_ref[h])
                gv_ref[rows, cols] = gv.astype(BF16)
        ck[i].start()
        cv[i].start()
    wait_all(ck + cv)


def gate_kernel(n, *refs):
    o_refs = refs[:n]
    gate_ref, grad_ref, gain_ref, gg_ref = refs[n:]
    wide = o_refs[0].shape[1]
    total = None
    for r in o_refs:
        o = r[...].astype(F32)
        s = jnp.sum(o * o, axis=1, keepdims=True)
        total = s if total is None else total + s
    inv = lax.rsqrt(total / (n * wide) + EPS)
    for k in range(n):
        cols = pl.ds(pl.multiple_of(partner(n, k, -1) * wide, wide), wide)
        g = gate_ref[:, cols].astype(F32)
        s = jax.nn.sigmoid(g)
        scaled = grad_ref[:, cols].astype(F32) * gain_ref[:, cols]
        normed = o_refs[k][...].astype(F32) * inv
        gg_ref[:, cols] = (scaled * normed * s * (1.0 + g * (1.0 - s))).astype(BF16)


def on_device(query, key_in, value, gate, gain, grad_out):
    d = HEAD_DIM
    t, own = query.shape
    heads = own // d
    rows, width = gate.shape
    n_seq, n_head = lax.axis_size("seq"), lax.axis_size("head")
    pairs = heads // 2
    gain = gain.reshape(1, width)

    def sds(shape, dtype):
        return jax.ShapeDtypeStruct(shape, dtype)

    def dma(n):
        return pltpu.SemaphoreType.DMA((n,))

    anywhere = pl.BlockSpec(memory_space=pl.ANY)
    whole = pl.BlockSpec(memory_space=pltpu.VMEM)
    wide = pl.BlockSpec((t, 2 * d), lambda i: (0, i))
    square = pl.BlockSpec((2, d, d), lambda i: (i, 0, 0))
    small = 2 * t * d * d * heads
    large = 2 * t * t * d * heads
    query, key_in, value = in_hbm(query), in_hbm(key_in), in_hbm(value)
    full = pltpu.VMEM((t, own), BF16)
    full32 = pltpu.VMEM((t, own), F32)

    def exchange(states, reverse):
        piece = (n_seq, heads * d // n_seq, d)
        states = lax.all_to_all(states.reshape(piece), "seq", 0, 0, tiled=True)
        summed = pl.pallas_call(
            functools.partial(running_kernel, reverse),
            out_shape=sds(piece, BF16),
            compiler_params=params(),
            cost_estimate=cost(heads * d * d, 4 * heads * d * d),
            name="running",
        )(states)
        return lax.all_to_all(summed, "seq", 0, 0, tiled=True).reshape(heads, d, d)

    states = pl.pallas_call(
        state_kernel,
        out_shape=sds((heads, d, d), BF16),
        in_specs=[anywhere, anywhere],
        out_specs=whole,
        scratch_shapes=[full, full, dma(2 * pairs)],
        compiler_params=params(),
        cost_estimate=cost(2 * small, 4 * t * own),
        name="states",
    )(key_in, value)
    prefix = exchange(states, False)

    weighted = pl.pallas_call(
        weigh_kernel,
        out_shape=[sds((rows, own), BF16)] * n_head,
        compiler_params=params(),
        cost_estimate=cost(20 * rows * width, 6 * rows * width),
        name="weigh",
    )(gate, grad_out, gain)
    weighted = [in_hbm(w) for w in send_all(weighted)]

    intra = pl.pallas_call(
        intra_kernel,
        out_shape=pltpu.HBM((t, own), F32),
        grid=(pairs,),
        in_specs=[wide, wide, wide],
        out_specs=wide,
        compiler_params=params(),
        cost_estimate=cost(2 * large, 10 * t * own),
        name="intra",
    )(query, key_in, value)

    tile = (n_head, 2 * t // d, d)
    sums, *out = pl.pallas_call(
        functools.partial(out_kernel, n_head),
        out_shape=[sds(tile, F32)] + [pltpu.HBM((rows, own), BF16)] * n_head,
        in_specs=[anywhere, anywhere, whole] + [anywhere] * n_head,
        out_specs=[whole] + [anywhere] * n_head,
        scratch_shapes=[
            full32, full, full, full, pltpu.VMEM((t, d), F32), pltpu.VMEM((t, d), F32),
            dma(2 * pairs + n_head), dma(n_head),
        ],
        compiler_params=params(),
        cost_estimate=cost(small, 10 * t * own),
        name="outs",
    )(in_hbm(intra), query, prefix, *weighted)
    sums = lax.all_to_all(sums, "head", 0, 0, tiled=True)

    states, grad_attn = pl.pallas_call(
        functools.partial(grad_kernel, n_head, float(width)),
        out_shape=[sds((heads, d, d), BF16), pltpu.HBM((t, own), BF16)],
        in_specs=[whole, anywhere] + [anywhere] * (2 * n_head),
        out_specs=[whole, anywhere],
        scratch_shapes=[full, full, full, full, dma(2 * n_head + pairs), dma(pairs)],
        compiler_params=params(),
        cost_estimate=cost(small, 8 * t * own),
        name="grads",
    )(sums, query, *weighted, *[in_hbm(o) for o in out])
    suffix = exchange(states, True)

    token_rows = send_all(out)
    grad_gate = pl.pallas_call(
        functools.partial(gate_kernel, n_head),
        out_shape=sds((rows, width), BF16),
        compiler_params=params(),
        cost_estimate=cost(20 * rows * width, 8 * rows * width),
        name="gates",
    )(*token_rows, gate, grad_out, gain)

    grad_query, part_key, part_value = pl.pallas_call(
        back_kernel,
        out_shape=[sds((t, own), BF16), pltpu.HBM((t, own), F32), pltpu.HBM((t, own), F32)],
        grid=(pairs,),
        in_specs=[wide, wide, wide, wide, square],
        out_specs=[wide, wide, wide],
        compiler_params=params(),
        cost_estimate=cost(4 * large, 18 * t * own),
        name="backs",
    )(query, key_in, value, in_hbm(grad_attn), prefix)

    grad_key, grad_value = pl.pallas_call(
        last_kernel,
        out_shape=[sds((t, own), BF16), sds((t, own), BF16)],
        in_specs=[anywhere] * 4 + [whole],
        out_specs=[anywhere] * 2,
        scratch_shapes=[full32, full32, full, full, full, full, dma(4 * pairs), dma(2 * pairs)],
        compiler_params=params(),
        cost_estimate=cost(2 * small, 16 * t * own),
        name="last",
    )(in_hbm(part_key), in_hbm(part_value), key_in, value, suffix)
    return grad_query, grad_key, grad_value, grad_gate


def solution(mesh):
    in_specs = (
        P("seq", "head"),
        P("seq", "head"),
        P("seq", "head"),
        P(("seq", "head"), None),
        P(),
        P(("seq", "head"), None),
    )
    out_specs = (P("seq", "head"), P("seq", "head"), P("seq", "head"), P(("seq", "head"), None))
    return jax.shard_map(
        on_device, mesh=mesh, in_specs=in_specs, out_specs=out_specs, check_vma=False
    )
```

```python
import functools

import jax
import jax.numpy as jnp
from jax import lax
from jax.experimental import pallas as pl
from jax.experimental.pallas import tpu as pltpu
from jax.sharding import PartitionSpec as P

HEAD_DIM = 128
EPS = 1e-06
F32 = jnp.float32
BF16 = jnp.bfloat16


def mm(a, b):
    return lax.dot_general(a, b, (((1,), (0,)), ((), ())), preferred_element_type=F32)


def mm_bt(a, b):
    return lax.dot_general(a, b, (((1,), (1,)), ((), ())), preferred_element_type=F32)


def mm_at(a, b):
    return lax.dot_general(a, b, (((0,), (0,)), ((), ())), preferred_element_type=F32)


def params():
    return pltpu.CompilerParams(vmem_limit_bytes=24 * 2**20)


def cost(flops, nbytes):
    return pl.CostEstimate(flops=int(flops), bytes_accessed=int(nbytes), transcendentals=0)


def in_hbm(x):
    return pltpu.with_memory_space_constraint(x, pltpu.HBM)


def in_vmem(x):
    return pltpu.with_memory_space_constraint(x, pltpu.VMEM)


def place(n, dx, dc, sign):
    me = lax.axis_index("head")
    chip, core = me // 2, me % 2
    flip = core + dc - 2 * core * dc
    return lax.rem(chip + sign * dx + n // 2, n // 2) * 2 + flip


def send_all(bundles):
    n = 2 * len(bundles)
    same = [bundles[0]]
    for dx in range(1, n // 2):
        pairs = [(i, (i + 2 * dx) % n) for i in range(n)]
        same.append(lax.ppermute(bundles[dx], "head", pairs))
    other = [lax.ppermute(b, "head", [(i, i ^ 1) for i in range(n)]) for b in same]
    return same + other


def parts(n):
    return [(dx + dc * (n // 2), dx, dc) for dx in range(n // 2) for dc in range(2)]


def start_all(copies):
    for c in copies:
        c.start()
    return copies


def wait_all(copies):
    for c in copies:
        c.wait()


def columns(i):
    return pl.ds(2 * HEAD_DIM * i, 2 * HEAD_DIM)


def by_pairs(src, dst, sems, at):
    n = src.shape[1] // (2 * HEAD_DIM)
    return [
        pltpu.make_async_copy(src.at[:, columns(i)], dst.at[:, columns(i)], sems.at[at + i])
        for i in range(n)
    ]


def rows_of(n, dx, dc, sign, rows):
    return pl.ds(pl.multiple_of(place(n, dx, dc, sign) * rows, rows), rows)


def assemble(n, bundles, dst, sems, at):
    rows = bundles[0].shape[1]
    return [
        pltpu.make_async_copy(
            bundles[k].at[dc], dst.at[rows_of(n, dx, dc, -1, rows), :], sems.at[at + i]
        )
        for i, (k, dx, dc) in enumerate(parts(n))
    ]


def state_kernel(a_hbm, b_hbm, s_ref, a_ref, b_ref, sems):
    d = HEAD_DIM
    n = s_ref.shape[0] // 2
    ca, cb = by_pairs(a_hbm, a_ref, sems, 0), by_pairs(b_hbm, b_ref, sems, n)
    for i in range(n):
        ca[i].start()
        cb[i].start()
    for i in range(n):
        ca[i].wait()
        cb[i].wait()
        for h in range(2 * i, 2 * i + 2):
            cols = slice(h * d, (h + 1) * d)
            s_ref[h] = mm_at(a_ref[:, cols], b_ref[:, cols]).astype(s_ref.dtype)


def running_kernel(reverse, x_ref, *refs):
    o_ref = refs[-1]
    n = x_ref.shape[0]
    total = jnp.zeros(x_ref.shape[1:], F32)
    for k in range(n):
        at = n - 1 - k if reverse else k
        o_ref[at] = total.astype(o_ref.dtype)
        total = total + x_ref[at].astype(F32)


def weigh_kernel(n, gate_ref, grad_ref, gain_ref, *w_refs):
    own = gate_ref.shape[1] // n
    for dx in range(n // 2):
        for dc in range(2):
            cols = pl.ds(pl.multiple_of(place(n, dx, dc, 1) * own, own), own)
            g = gate_ref[:, cols].astype(F32)
            w = grad_ref[:, cols].astype(F32) * gain_ref[:, cols] * g * jax.nn.sigmoid(g)
            w_refs[dx][dc] = w.astype(BF16)


def lower(n):
    return lax.broadcasted_iota(jnp.int32, (n, n), 0) >= lax.broadcasted_iota(jnp.int32, (n, n), 1)


def upper(n):
    return lax.broadcasted_iota(jnp.int32, (n, n), 0) <= lax.broadcasted_iota(jnp.int32, (n, n), 1)


def intra_kernel(q_hbm, k_hbm, v_hbm, _, i_hbm, s_hbm, *refs):
    q_ref, k_ref, v_ref, i_ref, s_ref, sems, out_sems = refs
    t, own = q_ref.shape
    half = t // 2
    n = own // (2 * HEAD_DIM)
    ins = [
        by_pairs(src, dst, sems, n * j)
        for j, (src, dst) in enumerate(((q_hbm, q_ref), (k_hbm, k_ref), (v_hbm, v_ref)))
    ]
    for i in range(n):
        for c in ins:
            c[i].start()
    outs = [
        pltpu.make_async_copy(s_ref.at[pl.ds(2 * i, 2)], s_hbm.at[pl.ds(2 * i, 2)], out_sems.at[i])
        for i in range(n)
    ]
    more = by_pairs(i_ref, i_hbm, out_sems, n)
    keep = lower(half)
    one, two = slice(0, half), slice(half, t)
    for i in range(n):
        for c in ins:
            c[i].wait()
        for h in range(2 * i, 2 * i + 2):
            cols = slice(h * HEAD_DIM, (h + 1) * HEAD_DIM)
            q, k, v = q_ref[:, cols], k_ref[:, cols], v_ref[:, cols]
            s0 = jnp.where(keep, mm_bt(q[one], k[one]), 0.0).astype(BF16)
            i_ref[one, cols] = mm(s0, v[one])
            s2 = mm_bt(q[two], k[one]).astype(BF16)
            s1 = jnp.where(keep, mm_bt(q[two], k[two]), 0.0).astype(BF16)
            i_ref[two, cols] = mm(s2, v[one]) + mm(s1, v[two])
            s_ref[h, 0], s_ref[h, 1], s_ref[h, 2] = s0, s1, s2
        outs[i].start()
        more[i].start()
    wait_all(outs + more)


def out_kernel(n_head, *refs):
    i_hbm, q_hbm, p_ref = refs[:3]
    w_any = refs[3 : 3 + n_head]
    sums_ref, o_ref, w_ref, q_ref = refs[3 + n_head : 7 + n_head]
    *bundles, i_ref, sems, out_sems = refs[7 + n_head :]
    d = HEAD_DIM
    t, own = q_ref.shape
    rows = t // n_head
    blocks = t // d
    cq = [
        pltpu.make_async_copy(q_hbm.at[pl.ds(r * d, d), :], q_ref.at[pl.ds(r * d, d), :], sems.at[r])
        for r in range(blocks)
    ]
    ci = [
        pltpu.make_async_copy(
            i_hbm.at[pl.ds(r * d, d), :], i_ref.at[pl.ds(r * d, d), :], sems.at[blocks + r]
        )
        for r in range(blocks)
    ]
    for r in range(blocks):
        cq[r].start()
        ci[r].start()
    cw = start_all(assemble(n_head, w_any, w_ref, sems, 2 * blocks))
    for r in range(blocks):
        at = slice(r * d, (r + 1) * d)
        cq[r].wait()
        ci[r].wait()
        for h in range(own // d):
            cols = slice(h * d, (h + 1) * d)
            o_ref[at, cols] = (i_ref[at, cols] + mm(q_ref[at, cols], p_ref[h])).astype(BF16)
    co = start_all(
        [
            pltpu.make_async_copy(
                o_ref.at[rows_of(n_head, dx, dc, 1, rows), :],
                bundles[dx].at[dc],
                out_sems.at[2 * dx + dc],
            )
            for dx in range(n_head // 2)
            for dc in range(2)
        ]
    )
    wait_all(cw)
    lines = [None] * (2 * blocks)
    for r in range(blocks):
        at = slice(r * d, (r + 1) * d)
        sq, cross = None, None
        for h in range(own // d):
            cols = slice(h * d, (h + 1) * d)
            o = o_ref[at, cols].astype(F32)
            a, b = o * o, o * w_ref[at, cols].astype(F32)
            sq, cross = (a, b) if sq is None else (sq + a, cross + b)
        lines[r] = jnp.sum(jnp.transpose(sq), axis=0, keepdims=True)
        lines[blocks + r] = jnp.sum(jnp.transpose(cross), axis=0, keepdims=True)
    tile = jnp.concatenate(lines, axis=0)
    for k in range(n_head):
        sums_ref[k] = tile
    wait_all(co)


def grad_kernel(width, sums_ref, q_ref, w_ref, o_ref, z_ref, do_hbm, do_ref, sems):
    d = HEAD_DIM
    t, own = q_ref.shape
    tile = jnp.sum(sums_ref[...], axis=0)
    blocks = t // d
    turned = jnp.transpose(jnp.concatenate([tile] * (d // tile.shape[0]), axis=0))
    inv = lax.rsqrt(turned[:, :blocks] / width + EPS)
    fall = inv * inv * inv * (turned[:, blocks : 2 * blocks] / width)
    copies = []
    for r in range(blocks):
        at = slice(r * d, (r + 1) * d)
        a = jnp.broadcast_to(inv[:, r : r + 1], (d, d))
        b = jnp.broadcast_to(fall[:, r : r + 1], (d, d))
        for h in range(own // d):
            cols = slice(h * d, (h + 1) * d)
            do = a * w_ref[at, cols].astype(F32) - b * o_ref[at, cols].astype(F32)
            do_ref[at, cols] = do.astype(BF16)
        copies.append(
            pltpu.make_async_copy(
                do_ref.at[pl.ds(r * d, d), :], do_hbm.at[pl.ds(r * d, d), :], sems.at[r]
            )
        )
        copies[r].start()
    for h in range(own // d):
        cols = slice(h * d, (h + 1) * d)
        z_ref[h] = mm_at(q_ref[:, cols], do_ref[:, cols]).astype(z_ref.dtype)
    wait_all(copies)


def back_kernel(
    q_hbm, k_hbm, v_hbm, do_hbm, t_hbm, p_ref, ak_hbm, av_hbm, gq_hbm,
    q_ref, k_ref, v_ref, do_ref, t_ref, ak_ref, av_ref, gq_ref, sems, out_sems,
):
    t, own = q_ref.shape
    half = t // 2
    n = own // (2 * HEAD_DIM)
    ins = [
        by_pairs(src, dst, sems, n * j)
        for j, (src, dst) in enumerate(
            ((do_hbm, do_ref), (v_hbm, v_ref), (k_hbm, k_ref), (q_hbm, q_ref))
        )
    ]
    ins.append(
        [
            pltpu.make_async_copy(
                t_hbm.at[pl.ds(2 * i, 2)], t_ref.at[pl.ds(2 * i, 2)], sems.at[4 * n + i]
            )
            for i in range(n)
        ]
    )
    for i in range(n):
        for c in ins:
            c[i].start()
    outs = [
        by_pairs(src, dst, out_sems, n * j)
        for j, (src, dst) in enumerate(((gq_ref, gq_hbm), (ak_ref, ak_hbm), (av_ref, av_hbm)))
    ]
    low = lower(half)
    one, two = slice(0, half), slice(half, t)
    for i in range(n):
        for c in ins:
            c[i].wait()
        for h in range(2 * i, 2 * i + 2):
            cols = slice(h * HEAD_DIM, (h + 1) * HEAD_DIM)
            q, k, v, do = q_ref[:, cols], k_ref[:, cols], v_ref[:, cols], do_ref[:, cols]
            qt, dot = q.T, do.T
            base = mm_bt(do, p_ref[h])
            g0 = jnp.where(low, mm_bt(do[one], v[one]), 0.0).astype(BF16)
            gq_ref[one, cols] = (mm(g0, k[one]) + base[one]).astype(BF16)
            g2 = mm_bt(do[two], v[one]).astype(BF16)
            g1 = jnp.where(low, mm_bt(do[two], v[two]), 0.0).astype(BF16)
            gq_ref[two, cols] = (mm(g2, k[one]) + mm(g1, k[two]) + base[two]).astype(BF16)
            ak_ref[one, cols] = (mm(qt[:, one], g0) + mm(qt[:, two], g2)).astype(BF16).T
            ak_ref[two, cols] = mm(qt[:, two], g1).astype(BF16).T
            s0, s1, s2 = t_ref[h, 0], t_ref[h, 1], t_ref[h, 2]
            av_ref[one, cols] = (mm(dot[:, one], s0) + mm(dot[:, two], s2)).astype(BF16).T
            av_ref[two, cols] = mm(dot[:, two], s1).astype(BF16).T
        for c in outs:
            c[i].start()
    for c in outs:
        wait_all(c)


def last_kernel(
    ak_hbm, av_hbm, k_hbm, v_hbm, s_ref, gk_hbm, gv_hbm,
    ak_ref, av_ref, k_ref, v_ref, gk_ref, gv_ref, sems, out_sems,
):
    d = HEAD_DIM
    t, own = k_ref.shape
    n = own // (2 * d)
    ins = [
        by_pairs(src, dst, sems, n * j)
        for j, (src, dst) in enumerate(
            ((k_hbm, k_ref), (av_hbm, av_ref), (v_hbm, v_ref), (ak_hbm, ak_ref))
        )
    ]
    for i in range(n):
        for c in ins:
            c[i].start()
    ck, cv = by_pairs(gk_ref, gk_hbm, out_sems, 0), by_pairs(gv_ref, gv_hbm, out_sems, n)
    for i in range(n):
        for c in ins:
            c[i].wait()
        for h in range(2 * i, 2 * i + 2):
            cols = slice(h * d, (h + 1) * d)
            for r in range(0, t, 256):
                rows = slice(r, r + 256)
                gv = av_ref[rows, cols].astype(F32) + mm(k_ref[rows, cols], s_ref[h])
                gv_ref[rows, cols] = gv.astype(BF16)
                gk = ak_ref[rows, cols].astype(F32) + mm_bt(v_ref[rows, cols], s_ref[h])
                gk_ref[rows, cols] = gk.astype(BF16)
        cv[i].start()
        ck[i].start()
    wait_all(ck + cv)


def gate_kernel(n, *refs):
    *o_refs, gate_ref, grad_ref, gain_ref, gg_ref = refs
    wide = o_refs[0].shape[2]
    total = None
    for k, _, dc in parts(n):
        o = o_refs[k][dc].astype(F32)
        s = o * o
        total = s if total is None else total + s
    inv = lax.rsqrt(jnp.sum(total, axis=1, keepdims=True) / (n * wide) + EPS)
    for k, dx, dc in parts(n):
        cols = pl.ds(pl.multiple_of(place(n, dx, dc, -1) * wide, wide), wide)
        g = gate_ref[:, cols].astype(F32)
        s = jax.nn.sigmoid(g)
        scaled = grad_ref[:, cols].astype(F32) * gain_ref[:, cols]
        normed = o_refs[k][dc].astype(F32) * inv
        gg_ref[:, cols] = (scaled * normed * s * (1.0 + g * (1.0 - s))).astype(BF16)


def on_device(query, key_in, value, gate, gain, grad_out):
    d = HEAD_DIM
    t, own = query.shape
    heads = own // d
    rows, width = gate.shape
    n_seq, n_head = lax.axis_size("seq"), lax.axis_size("head")
    pairs, chips = heads // 2, n_head // 2
    gain = gain.reshape(1, width)

    def sds(shape, dtype):
        return jax.ShapeDtypeStruct(shape, dtype)

    def dma(n):
        return pltpu.SemaphoreType.DMA((n,))

    anywhere = pl.BlockSpec(memory_space=pl.ANY)
    whole = pl.BlockSpec(memory_space=pltpu.VMEM)
    small = 2 * t * d * d * heads
    large = 2 * t * t * d * heads
    full = pltpu.VMEM((t, own), BF16)
    full32 = pltpu.VMEM((t, own), F32)
    piece = (n_seq, heads * d // n_seq, d)

    def exchange(states):
        return lax.all_to_all(states.reshape(piece), "seq", 0, 0, tiled=True)

    def running(states, reverse, *after):
        return pl.pallas_call(
            functools.partial(running_kernel, reverse),
            out_shape=pltpu.HBM(piece, BF16),
            in_specs=[whole] + [anywhere] * len(after),
            out_specs=whole,
            compiler_params=params(),
            cost_estimate=cost(heads * d * d, 4 * heads * d * d),
            name="running",
        )(states, *after)

    query, key_in, value = in_hbm(query), in_hbm(key_in), in_hbm(value)
    states = pl.pallas_call(
        state_kernel,
        out_shape=sds((heads, d, d), BF16),
        in_specs=[anywhere, anywhere],
        out_specs=whole,
        scratch_shapes=[full, full, dma(2 * pairs)],
        compiler_params=params(),
        cost_estimate=cost(2 * small, 4 * t * own),
        name="states",
    )(key_in, value)
    received = exchange(states)

    bundle = (2, rows, own)
    weighted = pl.pallas_call(
        functools.partial(weigh_kernel, n_head),
        out_shape=[sds(bundle, BF16)] * chips,
        compiler_params=params(),
        cost_estimate=cost(20 * rows * width, 6 * rows * width),
        name="weigh",
    )(gate, grad_out, gain)
    weighted = [in_hbm(w) for w in send_all(weighted)]

    tiles = (heads, 3, t // 2, t // 2)
    intra, scores = pl.pallas_call(
        intra_kernel,
        out_shape=[pltpu.HBM((t, own), F32), pltpu.HBM(tiles, BF16)],
        in_specs=[anywhere] * 4,
        out_specs=[anywhere, anywhere],
        scratch_shapes=[full] * 3
        + [full32, pltpu.VMEM(tiles, BF16), dma(3 * pairs), dma(2 * pairs)],
        compiler_params=params(),
        cost_estimate=cost(2 * large, 16 * t * own),
        name="intra",
    )(query, key_in, value, states)
    intra, scores = in_hbm(intra), in_hbm(scores)

    prefix = exchange(running(received, False, intra)).reshape(heads, d, d)

    tile = (n_head, 2 * t // d, d)
    sums, out, weighted, queries, *bundles = pl.pallas_call(
        functools.partial(out_kernel, n_head),
        out_shape=[sds(tile, F32), full, full, full] + [pltpu.HBM(bundle, BF16)] * chips,
        in_specs=[anywhere, anywhere, whole] + [anywhere] * n_head,
        out_specs=[whole] * 4 + [anywhere] * chips,
        scratch_shapes=[full32, dma(2 * t // d + n_head), dma(n_head)],
        compiler_params=params(),
        cost_estimate=cost(small, 10 * t * own),
        name="outs",
    )(intra, query, prefix, *weighted)
    sums = lax.all_to_all(sums, "head", 0, 0, tiled=True)

    states, grad_attn = pl.pallas_call(
        functools.partial(grad_kernel, float(width)),
        out_shape=[sds((heads, d, d), BF16), pltpu.HBM((t, own), BF16)],
        in_specs=[whole] * 4,
        out_specs=[whole, anywhere],
        scratch_shapes=[full, dma(t // d)],
        compiler_params=params(),
        cost_estimate=cost(small, 8 * t * own),
        name="grads",
    )(sums, in_vmem(queries), in_vmem(weighted), in_vmem(out))
    received = exchange(states)

    part_key, part_value, grad_query = pl.pallas_call(
        back_kernel,
        out_shape=[pltpu.HBM((t, own), BF16)] * 2 + [sds((t, own), BF16)],
        in_specs=[anywhere] * 5 + [whole],
        out_specs=[anywhere] * 3,
        scratch_shapes=[full] * 4 + [pltpu.VMEM(tiles, BF16)] + [full] * 3
        + [dma(5 * pairs), dma(3 * pairs)],
        compiler_params=params(),
        cost_estimate=cost(3 * large, 20 * t * own),
        name="backs",
    )(query, key_in, value, in_hbm(grad_attn), scores, prefix)
    part_key, part_value = in_hbm(part_key), in_hbm(part_value)
    suffix = exchange(running(received, True, part_key)).reshape(heads, d, d)

    token_rows = send_all(bundles)
    grad_gate = pl.pallas_call(
        functools.partial(gate_kernel, n_head),
        out_shape=sds((rows, width), BF16),
        compiler_params=params(),
        cost_estimate=cost(20 * rows * width, 8 * rows * width),
        name="gates",
    )(*token_rows, gate, grad_out, gain)

    grad_key, grad_value = pl.pallas_call(
        last_kernel,
        out_shape=[sds((t, own), BF16), sds((t, own), BF16)],
        in_specs=[anywhere] * 4 + [whole],
        out_specs=[anywhere] * 2,
        scratch_shapes=[full] * 6 + [dma(4 * pairs), dma(2 * pairs)],
        compiler_params=params(),
        cost_estimate=cost(2 * small, 16 * t * own),
        name="last",
    )(part_key, part_value, key_in, value, suffix)
    return grad_query, grad_key, grad_value, grad_gate


def solution(mesh):
    in_specs = (
        P("seq", "head"),
        P("seq", "head"),
        P("seq", "head"),
        P(("seq", "head"), None),
        P(),
        P(("seq", "head"), None),
    )
    out_specs = (P("seq", "head"), P("seq", "head"), P("seq", "head"), P(("seq", "head"), None))
    return jax.shard_map(
        on_device, mesh=mesh, in_specs=in_specs, out_specs=out_specs, check_vma=False
    )
```

```python
import functools

import jax
import jax.numpy as jnp
from jax import lax
from jax.experimental import pallas as pl
from jax.experimental.pallas import tpu as pltpu
from jax.sharding import PartitionSpec as P

HEAD_DIM = 128
EPS = 1e-06
F32 = jnp.float32
BF16 = jnp.bfloat16


def mm(a, b):
    return lax.dot_general(a, b, (((1,), (0,)), ((), ())), preferred_element_type=F32)


def mm_bt(a, b):
    return lax.dot_general(a, b, (((1,), (1,)), ((), ())), preferred_element_type=F32)


def mm_at(a, b):
    return lax.dot_general(a, b, (((0,), (0,)), ((), ())), preferred_element_type=F32)


def params():
    return pltpu.CompilerParams(vmem_limit_bytes=24 * 2**20)


def cost(flops, nbytes):
    return pl.CostEstimate(flops=int(flops), bytes_accessed=int(nbytes), transcendentals=0)


def in_hbm(x):
    return pltpu.with_memory_space_constraint(x, pltpu.HBM)


def in_vmem(x):
    return pltpu.with_memory_space_constraint(x, pltpu.VMEM)


def place(n, dx, dc, sign):
    me = lax.axis_index("head")
    chip, core = me // 2, me % 2
    flip = core + dc - 2 * core * dc
    return lax.rem(chip + sign * dx + n // 2, n // 2) * 2 + flip


def send_all(bundles):
    n = 2 * len(bundles)
    same = [bundles[0]]
    for dx in range(1, n // 2):
        pairs = [(i, (i + 2 * dx) % n) for i in range(n)]
        same.append(lax.ppermute(bundles[dx], "head", pairs))
    other = [lax.ppermute(b, "head", [(i, i ^ 1) for i in range(n)]) for b in same]
    return same + other


def parts(n):
    return [(dx + dc * (n // 2), dx, dc) for dx in range(n // 2) for dc in range(2)]


def start_all(copies):
    for c in copies:
        c.start()
    return copies


def wait_all(copies):
    for c in copies:
        c.wait()


def columns(i):
    return pl.ds(2 * HEAD_DIM * i, 2 * HEAD_DIM)


def by_pairs(src, dst, sems, at):
    n = src.shape[1] // (2 * HEAD_DIM)
    return [
        pltpu.make_async_copy(src.at[:, columns(i)], dst.at[:, columns(i)], sems.at[at + i])
        for i in range(n)
    ]


def rows_of(n, dx, dc, sign, rows):
    return pl.ds(pl.multiple_of(place(n, dx, dc, sign) * rows, rows), rows)


def assemble(n, bundles, dst, sems, at):
    rows = bundles[0].shape[1]
    return [
        pltpu.make_async_copy(
            bundles[k].at[dc], dst.at[rows_of(n, dx, dc, -1, rows), :], sems.at[at + i]
        )
        for i, (k, dx, dc) in enumerate(parts(n))
    ]


def state_kernel(a_hbm, b_hbm, s_ref, a_ref, b_ref, sems):
    d = HEAD_DIM
    n = s_ref.shape[0] // 2
    ca, cb = by_pairs(a_hbm, a_ref, sems, 0), by_pairs(b_hbm, b_ref, sems, n)
    for i in range(n):
        ca[i].start()
        cb[i].start()
    for i in range(n):
        ca[i].wait()
        cb[i].wait()
        for h in range(2 * i, 2 * i + 2):
            cols = slice(h * d, (h + 1) * d)
            s_ref[h] = mm_at(a_ref[:, cols], b_ref[:, cols]).astype(s_ref.dtype)


def running_kernel(reverse, x_ref, *refs):
    o_ref = refs[-1]
    n = x_ref.shape[0]
    total = jnp.zeros(x_ref.shape[1:], F32)
    for k in range(n):
        at = n - 1 - k if reverse else k
        o_ref[at] = total.astype(o_ref.dtype)
        total = total + x_ref[at].astype(F32)


def weigh_kernel(n, gate_ref, grad_ref, gain_ref, *w_refs):
    own = gate_ref.shape[1] // n
    for dx in range(n // 2):
        for dc in range(2):
            cols = pl.ds(pl.multiple_of(place(n, dx, dc, 1) * own, own), own)
            g = gate_ref[:, cols].astype(F32)
            w = grad_ref[:, cols].astype(F32) * gain_ref[:, cols] * g * jax.nn.sigmoid(g)
            w_refs[dx][dc] = w.astype(BF16)


def lower(n):
    return lax.broadcasted_iota(jnp.int32, (n, n), 0) >= lax.broadcasted_iota(jnp.int32, (n, n), 1)


def upper(n):
    return lax.broadcasted_iota(jnp.int32, (n, n), 0) <= lax.broadcasted_iota(jnp.int32, (n, n), 1)


def intra_kernel(first, q_hbm, k_hbm, v_hbm, *refs):
    i_hbm, s_hbm, q_ref, k_ref, v_ref, i_ref, s_ref, sems, out_sems = refs[-9:]
    t, own = q_ref.shape
    half = t // 2
    n = own // (2 * HEAD_DIM)
    q_hbm, k_hbm, v_hbm = [
        x.at[:, pl.ds(first * HEAD_DIM, own)] for x in (q_hbm, k_hbm, v_hbm)
    ]
    ins = [
        by_pairs(src, dst, sems, n * j)
        for j, (src, dst) in enumerate(((q_hbm, q_ref), (k_hbm, k_ref), (v_hbm, v_ref)))
    ]
    for i in range(n):
        for c in ins:
            c[i].start()
    outs = [
        pltpu.make_async_copy(s_ref.at[pl.ds(2 * i, 2)], s_hbm.at[pl.ds(2 * i, 2)], out_sems.at[i])
        for i in range(n)
    ]
    more = by_pairs(i_ref, i_hbm, out_sems, n)
    keep = lower(half)
    one, two = slice(0, half), slice(half, t)
    for i in range(n):
        for c in ins:
            c[i].wait()
        pair = []
        for h in range(2 * i, 2 * i + 2):
            cols = slice(h * HEAD_DIM, (h + 1) * HEAD_DIM)
            q, k = q_ref[:, cols], k_ref[:, cols]
            s0 = jnp.where(keep, mm_bt(q[one], k[one]), 0.0).astype(BF16)
            s2 = mm_bt(q[two], k[one]).astype(BF16)
            s1 = jnp.where(keep, mm_bt(q[two], k[two]), 0.0).astype(BF16)
            pair.append((h, cols, s0, s1, s2))
        for h, cols, s0, s1, s2 in pair:
            v = v_ref[:, cols]
            i_ref[one, cols] = mm(s0, v[one])
            i_ref[two, cols] = mm(jnp.concatenate([s2, s1], axis=1), v)
            s_ref[h, 0], s_ref[h, 1], s_ref[h, 2] = s0, s1, s2
        outs[i].start()
        more[i].start()
    wait_all(outs + more)


def out_kernel(n_head, *refs):
    i0_hbm, i1_hbm, q_hbm, p_ref = refs[:4]
    refs = refs[1:]
    w_any = refs[3 : 3 + n_head]
    sums_ref, o_ref, w_ref, q_ref = refs[3 + n_head : 7 + n_head]
    *bundles, i_ref, sems, out_sems = refs[7 + n_head :]
    d = HEAD_DIM
    t, own = q_ref.shape
    rows = t // n_head
    blocks = t // d
    cq = [
        pltpu.make_async_copy(q_hbm.at[pl.ds(r * d, d), :], q_ref.at[pl.ds(r * d, d), :], sems.at[r])
        for r in range(blocks)
    ]
    some = i0_hbm.shape[1]
    ci = [
        pltpu.make_async_copy(
            src.at[pl.ds(r * d, d), :],
            i_ref.at[pl.ds(r * d, d), pl.ds(j * some, some)],
            sems.at[(1 + j) * blocks + r],
        )
        for r in range(blocks)
        for j, src in enumerate((i0_hbm, i1_hbm))
    ]
    for r in range(blocks):
        cq[r].start()
        start_all(ci[2 * r : 2 * r + 2])
    cw = start_all(assemble(n_head, w_any, w_ref, sems, 3 * blocks))
    for r in range(blocks):
        at = slice(r * d, (r + 1) * d)
        cq[r].wait()
        wait_all(ci[2 * r : 2 * r + 2])
        for h in range(own // d):
            cols = slice(h * d, (h + 1) * d)
            o_ref[at, cols] = (i_ref[at, cols] + mm(q_ref[at, cols], p_ref[h])).astype(BF16)
    co = start_all(
        [
            pltpu.make_async_copy(
                o_ref.at[rows_of(n_head, dx, dc, 1, rows), :],
                bundles[dx].at[dc],
                out_sems.at[2 * dx + dc],
            )
            for dx in range(n_head // 2)
            for dc in range(2)
        ]
    )
    wait_all(cw)
    lines = [None] * (2 * blocks)
    for r in range(blocks):
        at = slice(r * d, (r + 1) * d)
        sq, cross = None, None
        for h in range(own // d):
            cols = slice(h * d, (h + 1) * d)
            o = o_ref[at, cols].astype(F32)
            a, b = o * o, o * w_ref[at, cols].astype(F32)
            sq, cross = (a, b) if sq is None else (sq + a, cross + b)
        lines[r] = jnp.sum(jnp.transpose(sq), axis=0, keepdims=True)
        lines[blocks + r] = jnp.sum(jnp.transpose(cross), axis=0, keepdims=True)
    tile = jnp.concatenate(lines, axis=0)
    for k in range(n_head):
        sums_ref[k] = tile
    wait_all(co)


def grad_kernel(width, sums_ref, q_ref, w_ref, o_ref, z_ref, do_hbm, do_ref, sems):
    d = HEAD_DIM
    t, own = q_ref.shape
    tile = jnp.sum(sums_ref[...], axis=0)
    blocks = t // d
    turned = jnp.transpose(jnp.concatenate([tile] * (d // tile.shape[0]), axis=0))
    inv = lax.rsqrt(turned[:, :blocks] / width + EPS)
    fall = inv * inv * inv * (turned[:, blocks : 2 * blocks] / width)
    copies = []
    for r in range(blocks):
        at = slice(r * d, (r + 1) * d)
        a = jnp.broadcast_to(inv[:, r : r + 1], (d, d))
        b = jnp.broadcast_to(fall[:, r : r + 1], (d, d))
        for h in range(own // d):
            cols = slice(h * d, (h + 1) * d)
            do = a * w_ref[at, cols].astype(F32) - b * o_ref[at, cols].astype(F32)
            do_ref[at, cols] = do.astype(BF16)
        copies.append(
            pltpu.make_async_copy(
                do_ref.at[pl.ds(r * d, d), :], do_hbm.at[pl.ds(r * d, d), :], sems.at[r]
            )
        )
        copies[r].start()
    for h in range(own // d):
        cols = slice(h * d, (h + 1) * d)
        z_ref[h] = mm_at(q_ref[:, cols], do_ref[:, cols]).astype(z_ref.dtype)
    wait_all(copies)


def back_kernel(
    q_hbm, k_hbm, v_hbm, do_hbm, t0_hbm, t1_hbm, p_ref, *refs
):
    ak_hbm, av_hbm, gq_hbm, q_ref, k_ref, v_ref, do_ref, t_ref = refs[-13:-5]
    ak_ref, av_ref, gq_ref, sems, out_sems = refs[-5:]
    t, own = q_ref.shape
    half = t // 2
    n = own // (2 * HEAD_DIM)
    ins = [
        by_pairs(src, dst, sems, n * j)
        for j, (src, dst) in enumerate(
            ((do_hbm, do_ref), (v_hbm, v_ref), (k_hbm, k_ref), (q_hbm, q_ref))
        )
    ]
    ins.append(
        [
            pltpu.make_async_copy(
                src.at[pl.ds(2 * i, 2)], t_ref.at[pl.ds(j * n + 2 * i, 2)], sems.at[4 * n + j * n // 2 + i]
            )
            for j, src in enumerate((t0_hbm, t1_hbm))
            for i in range(n // 2)
        ]
    )
    for i in range(n):
        for c in ins:
            c[i].start()
    outs = [
        by_pairs(src, dst, out_sems, n * j)
        for j, (src, dst) in enumerate(((gq_ref, gq_hbm), (ak_ref, ak_hbm), (av_ref, av_hbm)))
    ]
    low = lower(half)
    one, two = slice(0, half), slice(half, t)
    for i in range(n):
        for c in ins:
            c[i].wait()
        pair = []
        for h in range(2 * i, 2 * i + 2):
            cols = slice(h * HEAD_DIM, (h + 1) * HEAD_DIM)
            v, do = v_ref[:, cols], do_ref[:, cols]
            g0 = jnp.where(low, mm_bt(do[one], v[one]), 0.0).astype(BF16)
            g2 = mm_bt(do[two], v[one]).astype(BF16)
            g1 = jnp.where(low, mm_bt(do[two], v[two]), 0.0).astype(BF16)
            pair.append((h, cols, g0, g1, g2))
        for h, cols, _, _, _ in pair:
            dot = do_ref[:, cols].T
            s0, s1, s2 = t_ref[h, 0], t_ref[h, 1], t_ref[h, 2]
            av = mm(dot, jnp.concatenate([s0, s2], axis=0))
            av_ref[one, cols] = av.astype(BF16).T
            av_ref[two, cols] = mm(dot[:, two], s1).astype(BF16).T
        for h, cols, g0, g1, g2 in pair:
            qt, kt, dot = q_ref[:, cols].T, k_ref[:, cols].T, do_ref[:, cols].T
            base = mm(p_ref[h], dot)
            gq_ref[one, cols] = (mm_bt(kt[:, one], g0) + base[:, one]).astype(BF16).T
            gq = mm_bt(kt, jnp.concatenate([g2, g1], axis=1)) + base[:, two]
            gq_ref[two, cols] = gq.astype(BF16).T
            ak = mm(qt, jnp.concatenate([g0, g2], axis=0))
            ak_ref[one, cols] = ak.astype(BF16).T
            ak_ref[two, cols] = mm(qt[:, two], g1).astype(BF16).T
        for c in outs:
            c[i].start()
    for c in outs:
        wait_all(c)


def last_kernel(
    ak_hbm, av_hbm, k_hbm, v_hbm, s_ref, gk_hbm, gv_hbm,
    ak_ref, av_ref, k_ref, v_ref, gk_ref, gv_ref, sems, out_sems,
):
    d = HEAD_DIM
    t, own = k_ref.shape
    n = own // (2 * d)
    ins = [
        by_pairs(src, dst, sems, n * j)
        for j, (src, dst) in enumerate(
            ((k_hbm, k_ref), (av_hbm, av_ref), (v_hbm, v_ref), (ak_hbm, ak_ref))
        )
    ]
    for i in range(n):
        for c in ins:
            c[i].start()
    ck, cv = by_pairs(gk_ref, gk_hbm, out_sems, 0), by_pairs(gv_ref, gv_hbm, out_sems, n)
    for i in range(n):
        for c in ins:
            c[i].wait()
        for h in range(2 * i, 2 * i + 2):
            cols = slice(h * d, (h + 1) * d)
            for r in range(0, t, 256):
                rows = slice(r, r + 256)
                gv = av_ref[rows, cols].astype(F32) + mm(k_ref[rows, cols], s_ref[h])
                gv_ref[rows, cols] = gv.astype(BF16)
                gk = ak_ref[rows, cols].astype(F32) + mm_bt(v_ref[rows, cols], s_ref[h])
                gk_ref[rows, cols] = gk.astype(BF16)
        cv[i].start()
        ck[i].start()
    wait_all(ck + cv)


def gate_kernel(n, *refs):
    *o_refs, gate_ref, grad_ref, gain_ref, gg_ref = refs
    wide = o_refs[0].shape[2]
    total = None
    for k, _, dc in parts(n):
        o = o_refs[k][dc].astype(F32)
        s = o * o
        total = s if total is None else total + s
    inv = lax.rsqrt(jnp.sum(total, axis=1, keepdims=True) / (n * wide) + EPS)
    for k, dx, dc in parts(n):
        cols = pl.ds(pl.multiple_of(place(n, dx, dc, -1) * wide, wide), wide)
        g = gate_ref[:, cols].astype(F32)
        s = jax.nn.sigmoid(g)
        scaled = grad_ref[:, cols].astype(F32) * gain_ref[:, cols]
        normed = o_refs[k][dc].astype(F32) * inv
        gg_ref[:, cols] = (scaled * normed * s * (1.0 + g * (1.0 - s))).astype(BF16)


def on_device(query, key_in, value, gate, gain, grad_out):
    d = HEAD_DIM
    t, own = query.shape
    heads = own // d
    rows, width = gate.shape
    n_seq, n_head = lax.axis_size("seq"), lax.axis_size("head")
    pairs, chips = heads // 2, n_head // 2
    gain = gain.reshape(1, width)

    def sds(shape, dtype):
        return jax.ShapeDtypeStruct(shape, dtype)

    def dma(n):
        return pltpu.SemaphoreType.DMA((n,))

    anywhere = pl.BlockSpec(memory_space=pl.ANY)
    whole = pl.BlockSpec(memory_space=pltpu.VMEM)
    small = 2 * t * d * d * heads
    large = 2 * t * t * d * heads
    full = pltpu.VMEM((t, own), BF16)
    full32 = pltpu.VMEM((t, own), F32)
    piece = (n_seq, heads * d // n_seq, d)

    def exchange(states):
        return lax.all_to_all(states.reshape(piece), "seq", 0, 0, tiled=True)

    def running(states, reverse, *after):
        return pl.pallas_call(
            functools.partial(running_kernel, reverse),
            out_shape=pltpu.HBM(piece, BF16),
            in_specs=[whole] + [anywhere] * len(after),
            out_specs=whole,
            compiler_params=params(),
            cost_estimate=cost(heads * d * d, 4 * heads * d * d),
            name="running",
        )(states, *after)

    query, key_in, value = in_hbm(query), in_hbm(key_in), in_hbm(value)
    states = pl.pallas_call(
        state_kernel,
        out_shape=sds((heads, d, d), BF16),
        in_specs=[anywhere, anywhere],
        out_specs=whole,
        scratch_shapes=[full, full, dma(2 * pairs)],
        compiler_params=params(),
        cost_estimate=cost(2 * small, 4 * t * own),
        name="states",
    )(key_in, value)
    received = exchange(states)

    bundle = (2, rows, own)
    weighted = pl.pallas_call(
        functools.partial(weigh_kernel, n_head),
        out_shape=[sds(bundle, BF16)] * chips,
        compiler_params=params(),
        cost_estimate=cost(20 * rows * width, 6 * rows * width),
        name="weigh",
    )(gate, grad_out, gain)
    own_bundle = weighted[0]
    weighted = [in_hbm(w) for w in send_all(weighted)]

    tiles = (heads, 3, t // 2, t // 2)
    some = heads // 2
    tiles = (some, 3, t // 2, t // 2)

    def intra(first, *after):
        part = pltpu.VMEM((t, own // 2), BF16)
        inner, scores = pl.pallas_call(
            functools.partial(intra_kernel, first),
            out_shape=[pltpu.HBM((t, own // 2), F32), pltpu.HBM(tiles, BF16)],
            in_specs=[anywhere] * (3 + len(after)),
            out_specs=[anywhere, anywhere],
            scratch_shapes=[part] * 3
            + [pltpu.VMEM((t, own // 2), F32), pltpu.VMEM(tiles, BF16), dma(3 * some), dma(2 * some)],
            compiler_params=params(),
            cost_estimate=cost(large, 8 * t * own),
            name="intra",
        )(query, key_in, value, *after)
        return in_hbm(inner), in_hbm(scores)

    inner0, scores0 = intra(0, states)
    summed = running(received, False, own_bundle, inner0)
    prefix = exchange(summed).reshape(heads, d, d)
    inner1, scores1 = intra(some, in_hbm(summed), *weighted[1:chips])

    tile = (n_head, 2 * t // d, d)
    sums, out, weighted, queries, *bundles = pl.pallas_call(
        functools.partial(out_kernel, n_head),
        out_shape=[sds(tile, F32), full, full, full] + [pltpu.HBM(bundle, BF16)] * chips,
        in_specs=[anywhere] * 3 + [whole] + [anywhere] * n_head,
        out_specs=[whole] * 4 + [anywhere] * chips,
        scratch_shapes=[full32, dma(3 * t // d + n_head), dma(n_head)],
        compiler_params=params(),
        cost_estimate=cost(small, 10 * t * own),
        name="outs",
    )(inner0, inner1, query, prefix, *weighted)
    sums = lax.all_to_all(sums, "head", 0, 0, tiled=True)

    states, grad_attn = pl.pallas_call(
        functools.partial(grad_kernel, float(width)),
        out_shape=[sds((heads, d, d), BF16), pltpu.HBM((t, own), BF16)],
        in_specs=[whole] * 4,
        out_specs=[whole, anywhere],
        scratch_shapes=[full, dma(t // d)],
        compiler_params=params(),
        cost_estimate=cost(small, 8 * t * own),
        name="grads",
    )(sums, in_vmem(queries), in_vmem(weighted), in_vmem(out))
    received = exchange(states)

    part_key, part_value, grad_query = pl.pallas_call(
        back_kernel,
        out_shape=[pltpu.HBM((t, own), BF16)] * 2 + [sds((t, own), BF16)],
        in_specs=[anywhere] * 6 + [whole],
        out_specs=[anywhere] * 3,
        scratch_shapes=[full] * 4 + [pltpu.VMEM((heads,) + tiles[1:], BF16)] + [full] * 3
        + [dma(5 * pairs), dma(3 * pairs)],
        compiler_params=params(),
        cost_estimate=cost(3 * large, 20 * t * own),
        name="backs",
    )(query, key_in, value, in_hbm(grad_attn), scores0, scores1, prefix)
    part_key, part_value = in_hbm(part_key), in_hbm(part_value)
    suffix = exchange(running(received, True, part_key)).reshape(heads, d, d)

    token_rows = send_all(bundles)
    grad_gate = pl.pallas_call(
        functools.partial(gate_kernel, n_head),
        out_shape=sds((rows, width), BF16),
        compiler_params=params(),
        cost_estimate=cost(20 * rows * width, 8 * rows * width),
        name="gates",
    )(*token_rows, in_vmem(gate), in_vmem(grad_out), gain)

    grad_key, grad_value = pl.pallas_call(
        last_kernel,
        out_shape=[sds((t, own), BF16), sds((t, own), BF16)],
        in_specs=[anywhere] * 4 + [whole],
        out_specs=[anywhere] * 2,
        scratch_shapes=[full] * 6 + [dma(4 * pairs), dma(2 * pairs)],
        compiler_params=params(),
        cost_estimate=cost(2 * small, 16 * t * own),
        name="last",
    )(part_key, part_value, key_in, value, suffix)
    return grad_query, grad_key, grad_value, grad_gate


def solution(mesh):
    in_specs = (
        P("seq", "head"),
        P("seq", "head"),
        P("seq", "head"),
        P(("seq", "head"), None),
        P(),
        P(("seq", "head"), None),
    )
    out_specs = (P("seq", "head"), P("seq", "head"), P("seq", "head"), P(("seq", "head"), None))
    return jax.shard_map(
        on_device, mesh=mesh, in_specs=in_specs, out_specs=out_specs, check_vma=False
    )
```

```python
import functools

import jax
import jax.numpy as jnp
from jax import lax
from jax.experimental import pallas as pl
from jax.experimental.pallas import tpu as pltpu
from jax.sharding import PartitionSpec as P

HEAD_DIM = 128
EPS = 1e-06
F32 = jnp.float32
BF16 = jnp.bfloat16


def mm(a, b):
    return lax.dot_general(a, b, (((1,), (0,)), ((), ())), preferred_element_type=F32)


def mm_bt(a, b):
    return lax.dot_general(a, b, (((1,), (1,)), ((), ())), preferred_element_type=F32)


def mm_at(a, b):
    return lax.dot_general(a, b, (((0,), (0,)), ((), ())), preferred_element_type=F32)


def params():
    return pltpu.CompilerParams(vmem_limit_bytes=24 * 2**20)


def cost(flops, nbytes):
    return pl.CostEstimate(flops=int(flops), bytes_accessed=int(nbytes), transcendentals=0)


def in_hbm(x):
    return pltpu.with_memory_space_constraint(x, pltpu.HBM)


def in_vmem(x):
    return pltpu.with_memory_space_constraint(x, pltpu.VMEM)


def place(n, dx, dc, sign):
    me = lax.axis_index("head")
    chip, core = me // 2, me % 2
    flip = core + dc - 2 * core * dc
    return lax.rem(chip + sign * dx + n // 2, n // 2) * 2 + flip


def across(bundles):
    n = 2 * len(bundles)
    return [bundles[0]] + [
        lax.ppermute(bundles[dx], "head", [(i, (i + 2 * dx) % n) for i in range(n)])
        for dx in range(1, n // 2)
    ]


def send_all(bundles):
    n = 2 * len(bundles)
    same = across(bundles)
    return same + [lax.ppermute(b, "head", [(i, i ^ 1) for i in range(n)]) for b in same]


def parts(n):
    return [(dx + dc * (n // 2), dx, dc) for dx in range(n // 2) for dc in range(2)]


def start_all(copies):
    for c in copies:
        c.start()
    return copies


def wait_all(copies):
    for c in copies:
        c.wait()


def columns(i):
    return pl.ds(2 * HEAD_DIM * i, 2 * HEAD_DIM)


def by_pairs(src, dst, sems, at):
    n = src.shape[1] // (2 * HEAD_DIM)
    return [
        pltpu.make_async_copy(src.at[:, columns(i)], dst.at[:, columns(i)], sems.at[at + i])
        for i in range(n)
    ]


def rows_of(n, dx, dc, sign, rows):
    return pl.ds(pl.multiple_of(place(n, dx, dc, sign) * rows, rows), rows)


def assemble(n, bundles, dst, sems, at):
    rows = bundles[0].shape[1]
    return [
        pltpu.make_async_copy(
            bundles[k].at[dc], dst.at[rows_of(n, dx, dc, -1, rows), :], sems.at[at + i]
        )
        for i, (k, dx, dc) in enumerate(parts(n))
    ]


def state_kernel(a_hbm, b_hbm, s_ref, a_ref, b_ref, sems):
    d = HEAD_DIM
    n = s_ref.shape[0] // 2
    ca, cb = by_pairs(a_hbm, a_ref, sems, 0), by_pairs(b_hbm, b_ref, sems, n)
    for i in range(n):
        ca[i].start()
        cb[i].start()
    for i in range(n):
        ca[i].wait()
        cb[i].wait()
        for h in range(2 * i, 2 * i + 2):
            cols = slice(h * d, (h + 1) * d)
            s_ref[h] = mm_at(a_ref[:, cols], b_ref[:, cols]).astype(s_ref.dtype)


def running_kernel(reverse, x_ref, *refs):
    o_ref = refs[-1]
    n = x_ref.shape[0]
    total = jnp.zeros(x_ref.shape[1:], F32)
    for k in range(n):
        at = n - 1 - k if reverse else k
        o_ref[at] = total.astype(o_ref.dtype)
        total = total + x_ref[at].astype(F32)


def weigh_kernel(n, gate_ref, grad_ref, gain_ref, *w_refs):
    own = gate_ref.shape[1] // n
    for dx in range(n // 2):
        for dc in range(2):
            cols = pl.ds(pl.multiple_of(place(n, dx, dc, 1) * own, own), own)
            g = gate_ref[:, cols].astype(F32)
            w = grad_ref[:, cols].astype(F32) * gain_ref[:, cols] * g * jax.nn.sigmoid(g)
            w_refs[dx][dc] = w.astype(BF16)


def lower(n):
    return lax.broadcasted_iota(jnp.int32, (n, n), 0) >= lax.broadcasted_iota(jnp.int32, (n, n), 1)


def upper(n):
    return lax.broadcasted_iota(jnp.int32, (n, n), 0) <= lax.broadcasted_iota(jnp.int32, (n, n), 1)


def intra_kernel(first, q_hbm, k_hbm, v_hbm, *refs):
    i_hbm, s_hbm, q_ref, k_ref, v_ref, i_ref, s_ref, sems, out_sems = refs[-9:]
    t, own = q_ref.shape
    half = t // 2
    n = own // (2 * HEAD_DIM)
    q_hbm, k_hbm, v_hbm = [
        x.at[:, pl.ds(first * HEAD_DIM, own)] for x in (q_hbm, k_hbm, v_hbm)
    ]
    ins = [
        by_pairs(src, dst, sems, n * j)
        for j, (src, dst) in enumerate(((q_hbm, q_ref), (k_hbm, k_ref), (v_hbm, v_ref)))
    ]
    for i in range(n):
        for c in ins:
            c[i].start()
    outs = [
        pltpu.make_async_copy(s_ref.at[pl.ds(2 * i, 2)], s_hbm.at[pl.ds(2 * i, 2)], out_sems.at[i])
        for i in range(n)
    ]
    more = by_pairs(i_ref, i_hbm, out_sems, n)
    keep = lower(half)
    one, two = slice(0, half), slice(half, t)
    for i in range(n):
        for c in ins:
            c[i].wait()
        pair = []
        for h in range(2 * i, 2 * i + 2):
            cols = slice(h * HEAD_DIM, (h + 1) * HEAD_DIM)
            q, k = q_ref[:, cols], k_ref[:, cols]
            s0 = jnp.where(keep, mm_bt(q[one], k[one]), 0.0).astype(BF16)
            s2 = mm_bt(q[two], k[one]).astype(BF16)
            s1 = jnp.where(keep, mm_bt(q[two], k[two]), 0.0).astype(BF16)
            pair.append((h, cols, s0, s1, s2))
        for h, cols, s0, s1, s2 in pair:
            v = v_ref[:, cols]
            i_ref[one, cols] = mm(s0, v[one])
            i_ref[two, cols] = mm(jnp.concatenate([s2, s1], axis=1), v)
            s_ref[h, 0], s_ref[h, 1], s_ref[h, 2] = s0, s1, s2
        outs[i].start()
        more[i].start()
    wait_all(outs + more)


def out_kernel(n_head, *refs):
    i0_hbm, i1_hbm, q_hbm, p_ref = refs[:4]
    refs = refs[1:]
    w_any = refs[3 : 3 + n_head]
    sums_ref, o_ref, w_ref, q_ref = refs[3 + n_head : 7 + n_head]
    give_hbm, i_ref, sems, out_sems = refs[7 + n_head :]
    d = HEAD_DIM
    t, own = q_ref.shape
    rows = t // n_head
    blocks = t // d
    cq = [
        pltpu.make_async_copy(q_hbm.at[pl.ds(r * d, d), :], q_ref.at[pl.ds(r * d, d), :], sems.at[r])
        for r in range(blocks)
    ]
    some = i0_hbm.shape[1]
    ci = [
        pltpu.make_async_copy(
            src.at[pl.ds(r * d, d), :],
            i_ref.at[pl.ds(r * d, d), pl.ds(j * some, some)],
            sems.at[(1 + j) * blocks + r],
        )
        for r in range(blocks)
        for j, src in enumerate((i0_hbm, i1_hbm))
    ]
    for r in range(blocks):
        cq[r].start()
        start_all(ci[2 * r : 2 * r + 2])
    cw = start_all(assemble(n_head, w_any, w_ref, sems, 3 * blocks))
    for r in range(blocks):
        at = slice(r * d, (r + 1) * d)
        cq[r].wait()
        wait_all(ci[2 * r : 2 * r + 2])
        for h in range(own // d):
            cols = slice(h * d, (h + 1) * d)
            o_ref[at, cols] = (i_ref[at, cols] + mm(q_ref[at, cols], p_ref[h])).astype(BF16)
    co = start_all(
        [
            pltpu.make_async_copy(
                o_ref.at[rows_of(n_head, dx, 1, 1, rows), :], give_hbm.at[dx], out_sems.at[dx]
            )
            for dx in range(n_head // 2)
        ]
    )
    wait_all(cw)
    lines = [None] * (2 * blocks)
    for r in range(blocks):
        at = slice(r * d, (r + 1) * d)
        sq, cross = None, None
        for h in range(own // d):
            cols = slice(h * d, (h + 1) * d)
            o = o_ref[at, cols].astype(F32)
            a, b = o * o, o * w_ref[at, cols].astype(F32)
            sq, cross = (a, b) if sq is None else (sq + a, cross + b)
        lines[r] = jnp.sum(jnp.transpose(sq), axis=0, keepdims=True)
        lines[blocks + r] = jnp.sum(jnp.transpose(cross), axis=0, keepdims=True)
    tile = jnp.concatenate(lines, axis=0)
    for k in range(n_head):
        sums_ref[k] = tile
    wait_all(co)


def grad_kernel(n_head, width, sums_ref, q_ref, w_ref, o_ref, got_any, z_ref, do_hbm, *refs):
    *bundles, do_ref, sems, out_sems = refs
    rows = got_any.shape[1]
    ready = []
    for dx, bundle in enumerate(bundles):
        own_rows = o_ref.at[rows_of(n_head, dx, 0, 1, rows), :]
        ready.append(pltpu.make_async_copy(own_rows, bundle.at[0], out_sems.at[2 * dx]))
        ready.append(pltpu.make_async_copy(got_any.at[dx], bundle.at[1], out_sems.at[2 * dx + 1]))
    d = HEAD_DIM
    t, own = q_ref.shape
    tile = jnp.sum(sums_ref[...], axis=0)
    blocks = t // d
    turned = jnp.transpose(jnp.concatenate([tile] * (d // tile.shape[0]), axis=0))
    inv = lax.rsqrt(turned[:, :blocks] / width + EPS)
    fall = inv * inv * inv * (turned[:, blocks : 2 * blocks] / width)
    copies = []
    for r in range(blocks):
        at = slice(r * d, (r + 1) * d)
        a = jnp.broadcast_to(inv[:, r : r + 1], (d, d))
        b = jnp.broadcast_to(fall[:, r : r + 1], (d, d))
        for h in range(own // d):
            cols = slice(h * d, (h + 1) * d)
            do = a * w_ref[at, cols].astype(F32) - b * o_ref[at, cols].astype(F32)
            do_ref[at, cols] = do.astype(BF16)
        copies.append(
            pltpu.make_async_copy(
                do_ref.at[pl.ds(r * d, d), :], do_hbm.at[pl.ds(r * d, d), :], sems.at[r]
            )
        )
        copies[r].start()
        start_all(ready[r * len(ready) // blocks : (r + 1) * len(ready) // blocks])
    for h in range(own // d):
        cols = slice(h * d, (h + 1) * d)
        z_ref[h] = mm_at(q_ref[:, cols], do_ref[:, cols]).astype(z_ref.dtype)
    wait_all(copies + ready)


def back_kernel(
    q_hbm, k_hbm, v_hbm, do_hbm, t0_hbm, t1_hbm, p_ref, *refs
):
    ak_hbm, av_hbm, gq_hbm, q_ref, k_ref, v_ref, do_ref, t_ref = refs[-13:-5]
    ak_ref, av_ref, gq_ref, sems, out_sems = refs[-5:]
    t, own = q_ref.shape
    half = t // 2
    n = own // (2 * HEAD_DIM)
    ins = [
        by_pairs(src, dst, sems, n * j)
        for j, (src, dst) in enumerate(
            ((do_hbm, do_ref), (v_hbm, v_ref), (k_hbm, k_ref), (q_hbm, q_ref))
        )
    ]
    ins.append(
        [
            pltpu.make_async_copy(
                src.at[pl.ds(2 * i, 2)], t_ref.at[pl.ds(j * n + 2 * i, 2)], sems.at[4 * n + j * n // 2 + i]
            )
            for j, src in enumerate((t0_hbm, t1_hbm))
            for i in range(n // 2)
        ]
    )
    for i in range(n):
        for c in ins:
            c[i].start()
    outs = [
        by_pairs(src, dst, out_sems, n * j)
        for j, (src, dst) in enumerate(((gq_ref, gq_hbm), (ak_ref, ak_hbm), (av_ref, av_hbm)))
    ]
    low = lower(half)
    one, two = slice(0, half), slice(half, t)
    for i in range(n):
        for c in ins:
            c[i].wait()
        pair = []
        for h in range(2 * i, 2 * i + 2):
            cols = slice(h * HEAD_DIM, (h + 1) * HEAD_DIM)
            v, do = v_ref[:, cols], do_ref[:, cols]
            g0 = jnp.where(low, mm_bt(do[one], v[one]), 0.0).astype(BF16)
            g2 = mm_bt(do[two], v[one]).astype(BF16)
            g1 = jnp.where(low, mm_bt(do[two], v[two]), 0.0).astype(BF16)
            pair.append((h, cols, g0, g1, g2))
        for h, cols, _, _, _ in pair:
            dot = do_ref[:, cols].T
            s0, s1, s2 = t_ref[h, 0], t_ref[h, 1], t_ref[h, 2]
            av = mm(dot, jnp.concatenate([s0, s2], axis=0))
            av_ref[one, cols] = av.astype(BF16).T
            av_ref[two, cols] = mm(dot[:, two], s1).astype(BF16).T
        for h, cols, g0, g1, g2 in pair:
            qt, kt, dot = q_ref[:, cols].T, k_ref[:, cols].T, do_ref[:, cols].T
            base = mm(p_ref[h], dot)
            gq_ref[one, cols] = (mm_bt(kt[:, one], g0) + base[:, one]).astype(BF16).T
            gq = mm_bt(kt, jnp.concatenate([g2, g1], axis=1)) + base[:, two]
            gq_ref[two, cols] = gq.astype(BF16).T
            ak = mm(qt, jnp.concatenate([g0, g2], axis=0))
            ak_ref[one, cols] = ak.astype(BF16).T
            ak_ref[two, cols] = mm(qt[:, two], g1).astype(BF16).T
        for c in outs:
            c[i].start()
    for c in outs:
        wait_all(c)


def last_kernel(
    ak_hbm, av_hbm, k_ref, v_ref, s_ref, gk_hbm, gv_hbm,
    ak_ref, av_ref, gk_ref, gv_ref, sems, out_sems,
):
    d = HEAD_DIM
    t, own = k_ref.shape
    n = own // (2 * d)
    ins = [
        by_pairs(src, dst, sems, n * j)
        for j, (src, dst) in enumerate(
            ((av_hbm, av_ref), (ak_hbm, ak_ref))
        )
    ]
    for i in range(n):
        for c in ins:
            c[i].start()
    ck, cv = by_pairs(gk_ref, gk_hbm, out_sems, 0), by_pairs(gv_ref, gv_hbm, out_sems, n)
    for i in range(n):
        for c in ins:
            c[i].wait()
        for h in range(2 * i, 2 * i + 2):
            cols = slice(h * d, (h + 1) * d)
            for r in range(0, t, 256):
                rows = slice(r, r + 256)
                gv = av_ref[rows, cols].astype(F32) + mm(k_ref[rows, cols], s_ref[h])
                gv_ref[rows, cols] = gv.astype(BF16)
                gk = ak_ref[rows, cols].astype(F32) + mm_bt(v_ref[rows, cols], s_ref[h])
                gk_ref[rows, cols] = gk.astype(BF16)
        cv[i].start()
        ck[i].start()
    wait_all(ck + cv)


def gate_kernel(n, *refs):
    chips = n // 2
    srcs, gain_ref, gg_hbm = refs[: chips + 2], refs[chips + 2], refs[chips + 3]
    dsts, (gg_ref, sems, out_sems) = refs[chips + 4 : 2 * chips + 6], refs[2 * chips + 6 :]
    loads = start_all(
        [pltpu.make_async_copy(x, y, sems.at[j]) for j, (x, y) in enumerate(zip(srcs, dsts))]
    )
    *o_refs, gate_ref, grad_ref = dsts
    wide = o_refs[0].shape[2]
    total = None
    for dx in range(chips):
        loads[dx].wait()
        for dc in range(2):
            o = o_refs[dx][dc].astype(F32)
            o = jnp.sum(o * o, axis=1, keepdims=True)
            total = o if total is None else total + o
    inv = lax.rsqrt(total / (n * wide) + EPS)
    wait_all(loads[chips:])
    stores = []
    for dx in range(chips):
        for dc in range(2):
            cols = pl.ds(pl.multiple_of(place(n, dx, dc, -1) * wide, wide), wide)
            g = gate_ref[:, cols].astype(F32)
            s = jax.nn.sigmoid(g)
            scaled = grad_ref[:, cols].astype(F32) * gain_ref[:, cols]
            normed = o_refs[dx][dc].astype(F32) * inv
            gg_ref[:, cols] = (scaled * normed * s * (1.0 + g * (1.0 - s))).astype(BF16)
            store = pltpu.make_async_copy(
                gg_ref.at[:, cols], gg_hbm.at[:, cols], out_sems.at[2 * dx + dc]
            )
            store.start()
            stores.append(store)
    wait_all(stores)


def on_device(query, key_in, value, gate, gain, grad_out):
    d = HEAD_DIM
    t, own = query.shape
    heads = own // d
    rows, width = gate.shape
    n_seq, n_head = lax.axis_size("seq"), lax.axis_size("head")
    pairs, chips = heads // 2, n_head // 2
    gain = gain.reshape(1, width)

    def sds(shape, dtype):
        return jax.ShapeDtypeStruct(shape, dtype)

    def dma(n):
        return pltpu.SemaphoreType.DMA((n,))

    anywhere = pl.BlockSpec(memory_space=pl.ANY)
    whole = pl.BlockSpec(memory_space=pltpu.VMEM)
    small = 2 * t * d * d * heads
    large = 2 * t * t * d * heads
    full = pltpu.VMEM((t, own), BF16)
    full32 = pltpu.VMEM((t, own), F32)
    piece = (n_seq, heads * d // n_seq, d)

    def exchange(states):
        return lax.all_to_all(states.reshape(piece), "seq", 0, 0, tiled=True)

    def running(states, reverse, *after):
        return pl.pallas_call(
            functools.partial(running_kernel, reverse),
            out_shape=pltpu.HBM(piece, BF16),
            in_specs=[whole] + [anywhere] * len(after),
            out_specs=whole,
            compiler_params=params(),
            cost_estimate=cost(heads * d * d, 4 * heads * d * d),
            name="running",
        )(states, *after)

    keys, values = in_vmem(key_in), in_vmem(value)
    query, key_in, value = in_hbm(query), in_hbm(key_in), in_hbm(value)
    states = pl.pallas_call(
        state_kernel,
        out_shape=sds((heads, d, d), BF16),
        in_specs=[anywhere, anywhere],
        out_specs=whole,
        scratch_shapes=[full, full, dma(2 * pairs)],
        compiler_params=params(),
        cost_estimate=cost(2 * small, 4 * t * own),
        name="states",
    )(key_in, value)
    received = exchange(states)

    bundle = (2, rows, own)
    weighted = pl.pallas_call(
        functools.partial(weigh_kernel, n_head),
        out_shape=[sds(bundle, BF16)] * chips,
        compiler_params=params(),
        cost_estimate=cost(20 * rows * width, 6 * rows * width),
        name="weigh",
    )(gate, grad_out, gain)
    own_bundle = weighted[0]
    weighted = [in_hbm(w) for w in send_all(weighted)]

    tiles = (heads, 3, t // 2, t // 2)
    some = heads // 2
    tiles = (some, 3, t // 2, t // 2)

    def intra(first, *after):
        part = pltpu.VMEM((t, own // 2), BF16)
        inner, scores = pl.pallas_call(
            functools.partial(intra_kernel, first),
            out_shape=[pltpu.HBM((t, own // 2), F32), pltpu.HBM(tiles, BF16)],
            in_specs=[anywhere] * (3 + len(after)),
            out_specs=[anywhere, anywhere],
            scratch_shapes=[part] * 3
            + [pltpu.VMEM((t, own // 2), F32), pltpu.VMEM(tiles, BF16), dma(3 * some), dma(2 * some)],
            compiler_params=params(),
            cost_estimate=cost(large, 8 * t * own),
            name="intra",
        )(query, key_in, value, *after)
        return in_hbm(inner), in_hbm(scores)

    inner0, scores0 = intra(0, states)
    summed = running(received, False, own_bundle, inner0)
    prefix = exchange(summed).reshape(heads, d, d)
    inner1, scores1 = intra(some, in_hbm(summed), *weighted[1:chips])

    tile = (n_head, 2 * t // d, d)
    sums, out, weighted, queries, given = pl.pallas_call(
        functools.partial(out_kernel, n_head),
        out_shape=[sds(tile, F32), full, full, full, pltpu.HBM((chips, rows, own), BF16)],
        in_specs=[anywhere] * 3 + [whole] + [anywhere] * n_head,
        out_specs=[whole] * 4 + [anywhere],
        scratch_shapes=[full32, dma(3 * t // d + n_head), dma(chips)],
        compiler_params=params(),
        cost_estimate=cost(small, 10 * t * own),
        name="outs",
    )(inner0, inner1, query, prefix, *weighted)
    sums = lax.all_to_all(sums, "head", 0, 0, tiled=True)

    got = lax.ppermute(given, "head", [(i, i ^ 1) for i in range(n_head)])
    states, grad_attn, *bundles = pl.pallas_call(
        functools.partial(grad_kernel, n_head, float(width)),
        out_shape=[sds((heads, d, d), BF16), pltpu.HBM((t, own), BF16)]
        + [pltpu.HBM(bundle, BF16)] * chips,
        in_specs=[whole] * 4 + [anywhere],
        out_specs=[whole] + [anywhere] * (1 + chips),
        scratch_shapes=[full, dma(t // d), dma(n_head)],
        compiler_params=params(),
        cost_estimate=cost(small, 8 * t * own),
        name="grads",
    )(sums, in_vmem(queries), in_vmem(weighted), in_vmem(out), got)
    received = exchange(states)

    part_key, part_value, grad_query = pl.pallas_call(
        back_kernel,
        out_shape=[pltpu.HBM((t, own), BF16)] * 2 + [sds((t, own), BF16)],
        in_specs=[anywhere] * 6 + [whole],
        out_specs=[anywhere] * 3,
        scratch_shapes=[full] * 4 + [pltpu.VMEM((heads,) + tiles[1:], BF16)] + [full] * 3
        + [dma(5 * pairs), dma(3 * pairs)],
        compiler_params=params(),
        cost_estimate=cost(3 * large, 20 * t * own),
        name="backs",
    )(query, key_in, value, in_hbm(grad_attn), scores0, scores1, prefix)
    part_key, part_value = in_hbm(part_key), in_hbm(part_value)
    suffix = exchange(running(received, True, part_key)).reshape(heads, d, d)

    token_rows = across(bundles)
    strip = pltpu.VMEM((rows, width), BF16)
    grad_gate = pl.pallas_call(
        functools.partial(gate_kernel, n_head),
        out_shape=sds((rows, width), BF16),
        in_specs=[anywhere] * (chips + 2) + [whole],
        out_specs=anywhere,
        scratch_shapes=[pltpu.VMEM(bundle, BF16)] * chips
        + [strip, strip, strip, dma(chips + 2), dma(n_head)],
        compiler_params=params(),
        cost_estimate=cost(30 * large, 200 * t * own),
        name="gates",
    )(in_hbm(token_rows[0]), *token_rows[1:], in_hbm(gate), in_hbm(grad_out), gain)

    grad_key, grad_value = pl.pallas_call(
        last_kernel,
        out_shape=[sds((t, own), BF16), sds((t, own), BF16)],
        in_specs=[anywhere] * 2 + [whole] * 3,
        out_specs=[anywhere] * 2,
        scratch_shapes=[full] * 4 + [dma(2 * pairs), dma(2 * pairs)],
        compiler_params=params(),
        cost_estimate=cost(2 * small, 16 * t * own),
        name="last",
    )(part_key, part_value, keys, values, suffix)
    return grad_query, grad_key, grad_value, grad_gate


def solution(mesh):
    in_specs = (
        P("seq", "head"),
        P("seq", "head"),
        P("seq", "head"),
        P(("seq", "head"), None),
        P(),
        P(("seq", "head"), None),
    )
    out_specs = (P("seq", "head"), P("seq", "head"), P("seq", "head"), P(("seq", "head"), None))
    return jax.shard_map(
        on_device, mesh=mesh, in_specs=in_specs, out_specs=out_specs, check_vma=False
    )
```

```python
import functools

import jax
import jax.numpy as jnp
from jax import lax
from jax.experimental import pallas as pl
from jax.experimental.pallas import tpu as pltpu
from jax.sharding import PartitionSpec as P

HEAD_DIM = 128
EPS = 1e-06
F32 = jnp.float32
BF16 = jnp.bfloat16


def mm(a, b):
    return lax.dot_general(a, b, (((1,), (0,)), ((), ())), preferred_element_type=F32)


def mm_bt(a, b):
    return lax.dot_general(a, b, (((1,), (1,)), ((), ())), preferred_element_type=F32)


def mm_at(a, b):
    return lax.dot_general(a, b, (((0,), (0,)), ((), ())), preferred_element_type=F32)


def params():
    return pltpu.CompilerParams(vmem_limit_bytes=24 * 2**20)


def cost(flops, nbytes):
    return pl.CostEstimate(flops=int(flops), bytes_accessed=int(nbytes), transcendentals=0)


def in_hbm(x):
    return pltpu.with_memory_space_constraint(x, pltpu.HBM)


def in_vmem(x):
    return pltpu.with_memory_space_constraint(x, pltpu.VMEM)


def place(n, dx, dc, sign):
    me = lax.axis_index("head")
    chip, core = me // 2, me % 2
    flip = core + dc - 2 * core * dc
    return lax.rem(chip + sign * dx + n // 2, n // 2) * 2 + flip


def across(bundles):
    n = 2 * len(bundles)
    return [bundles[0]] + [
        lax.ppermute(bundles[dx], "head", [(i, (i + 2 * dx) % n) for i in range(n)])
        for dx in range(1, n // 2)
    ]


def send_all(bundles):
    n = 2 * len(bundles)
    same = across(bundles)
    return same + [lax.ppermute(b, "head", [(i, i ^ 1) for i in range(n)]) for b in same]


def parts(n):
    return [(dx + dc * (n // 2), dx, dc) for dx in range(n // 2) for dc in range(2)]


def start_all(copies):
    for c in copies:
        c.start()
    return copies


def wait_all(copies):
    for c in copies:
        c.wait()


def columns(i):
    return pl.ds(2 * HEAD_DIM * i, 2 * HEAD_DIM)


def by_pairs(src, dst, sems, at):
    n = src.shape[1] // (2 * HEAD_DIM)
    return [
        pltpu.make_async_copy(src.at[:, columns(i)], dst.at[:, columns(i)], sems.at[at + i])
        for i in range(n)
    ]


def rows_of(n, dx, dc, sign, rows):
    return pl.ds(pl.multiple_of(place(n, dx, dc, sign) * rows, rows), rows)


def assemble(n, bundles, dst, sems, at):
    rows = bundles[0].shape[1]
    return [
        pltpu.make_async_copy(
            bundles[k].at[dc], dst.at[rows_of(n, dx, dc, -1, rows), :], sems.at[at + i]
        )
        for i, (k, dx, dc) in enumerate(parts(n))
    ]


def state_kernel(a_hbm, b_hbm, s_ref, a_ref, b_ref, sems):
    d = HEAD_DIM
    n = s_ref.shape[0] // 2
    ca, cb = by_pairs(a_hbm, a_ref, sems, 0), by_pairs(b_hbm, b_ref, sems, n)
    for i in range(n):
        ca[i].start()
        cb[i].start()
    for i in range(n):
        ca[i].wait()
        cb[i].wait()
        for h in range(2 * i, 2 * i + 2):
            cols = slice(h * d, (h + 1) * d)
            s_ref[h] = mm_at(a_ref[:, cols], b_ref[:, cols]).astype(s_ref.dtype)


def running_kernel(reverse, x_ref, *refs):
    o_ref = refs[-1]
    n = x_ref.shape[0]
    total = jnp.zeros(x_ref.shape[1:], F32)
    for k in range(n):
        at = n - 1 - k if reverse else k
        o_ref[at] = total.astype(o_ref.dtype)
        total = total + x_ref[at].astype(F32)


def weigh_kernel(n, gate_ref, grad_ref, gain_ref, *w_refs):
    own = gate_ref.shape[1] // n
    for dx in range(n // 2):
        for dc in range(2):
            cols = pl.ds(pl.multiple_of(place(n, dx, dc, 1) * own, own), own)
            g = gate_ref[:, cols].astype(F32)
            w = grad_ref[:, cols].astype(F32) * gain_ref[:, cols] * g * jax.nn.sigmoid(g)
            w_refs[dx][dc] = w.astype(BF16)


def lower(n):
    return lax.broadcasted_iota(jnp.int32, (n, n), 0) >= lax.broadcasted_iota(jnp.int32, (n, n), 1)


def upper(n):
    return lax.broadcasted_iota(jnp.int32, (n, n), 0) <= lax.broadcasted_iota(jnp.int32, (n, n), 1)


def intra_kernel(first, q_hbm, k_hbm, v_hbm, *refs):
    i_hbm, s_hbm, q_ref, k_ref, v_ref, i_ref, s_ref, sems, out_sems = refs[-9:]
    t, own = q_ref.shape
    half = t // 2
    n = own // (2 * HEAD_DIM)
    q_hbm, k_hbm, v_hbm = [
        x.at[:, pl.ds(first * HEAD_DIM, own)] for x in (q_hbm, k_hbm, v_hbm)
    ]
    ins = [
        by_pairs(src, dst, sems, n * j)
        for j, (src, dst) in enumerate(((q_hbm, q_ref), (k_hbm, k_ref), (v_hbm, v_ref)))
    ]
    for i in range(n):
        for c in ins:
            c[i].start()
    outs = [
        pltpu.make_async_copy(s_ref.at[pl.ds(2 * i, 2)], s_hbm.at[pl.ds(2 * i, 2)], out_sems.at[i])
        for i in range(n)
    ]
    more = by_pairs(i_ref, i_hbm, out_sems, n)
    keep = lower(half)
    one, two = slice(0, half), slice(half, t)
    for i in range(n):
        for c in ins:
            c[i].wait()
        pair = []
        for h in range(2 * i, 2 * i + 2):
            cols = slice(h * HEAD_DIM, (h + 1) * HEAD_DIM)
            q, k = q_ref[:, cols], k_ref[:, cols]
            s0 = jnp.where(keep, mm_bt(q[one], k[one]), 0.0).astype(BF16)
            s2 = mm_bt(q[two], k[one]).astype(BF16)
            s1 = jnp.where(keep, mm_bt(q[two], k[two]), 0.0).astype(BF16)
            pair.append((h, cols, s0, s1, s2))
        for h, cols, s0, s1, s2 in pair:
            v = v_ref[:, cols]
            i_ref[one, cols] = mm(s0, v[one])
            i_ref[two, cols] = mm(jnp.concatenate([s2, s1], axis=1), v)
            s_ref[h, 0], s_ref[h, 1], s_ref[h, 2] = s0, s1, s2
        outs[i].start()
        more[i].start()
    wait_all(outs + more)


def out_kernel(n_head, *refs):
    i0_hbm, i1_hbm, q_hbm, p_ref = refs[:4]
    refs = refs[1:]
    w_any = refs[3 : 3 + n_head]
    sums_ref, o_ref, w_ref, q_ref = refs[3 + n_head : 7 + n_head]
    give_hbm, i_ref, sems, out_sems = refs[7 + n_head :]
    d = HEAD_DIM
    t, own = q_ref.shape
    rows = t // n_head
    blocks = t // d
    cq = [
        pltpu.make_async_copy(q_hbm.at[pl.ds(r * d, d), :], q_ref.at[pl.ds(r * d, d), :], sems.at[r])
        for r in range(blocks)
    ]
    some = i0_hbm.shape[1]
    ci = [
        pltpu.make_async_copy(
            src.at[pl.ds(r * d, d), :],
            i_ref.at[pl.ds(r * d, d), pl.ds(j * some, some)],
            sems.at[(1 + j) * blocks + r],
        )
        for r in range(blocks)
        for j, src in enumerate((i0_hbm, i1_hbm))
    ]
    for r in range(blocks):
        cq[r].start()
        start_all(ci[2 * r : 2 * r + 2])
    cw = start_all(assemble(n_head, w_any, w_ref, sems, 3 * blocks))
    for r in range(blocks):
        at = slice(r * d, (r + 1) * d)
        cq[r].wait()
        wait_all(ci[2 * r : 2 * r + 2])
        for h in range(own // d):
            cols = slice(h * d, (h + 1) * d)
            o_ref[at, cols] = (i_ref[at, cols] + mm(q_ref[at, cols], p_ref[h])).astype(BF16)
    co = start_all(
        [
            pltpu.make_async_copy(
                o_ref.at[rows_of(n_head, dx, 1, 1, rows), :], give_hbm.at[dx], out_sems.at[dx]
            )
            for dx in range(n_head // 2)
        ]
    )
    wait_all(cw)
    lines = [None] * (2 * blocks)
    for r in range(blocks):
        at = slice(r * d, (r + 1) * d)
        sq, cross = None, None
        for h in range(own // d):
            cols = slice(h * d, (h + 1) * d)
            o = o_ref[at, cols].astype(F32)
            a, b = o * o, o * w_ref[at, cols].astype(F32)
            sq, cross = (a, b) if sq is None else (sq + a, cross + b)
        lines[r] = jnp.sum(jnp.transpose(sq), axis=0, keepdims=True)
        lines[blocks + r] = jnp.sum(jnp.transpose(cross), axis=0, keepdims=True)
    tile = jnp.concatenate(lines, axis=0)
    for k in range(n_head):
        sums_ref[k] = tile
    wait_all(co)


def grad_kernel(n_head, width, sums_ref, q_ref, w_ref, o_ref, got_any, z_ref, do_hbm, *refs):
    *bundles, do_ref, sems, out_sems = refs
    rows = got_any.shape[1]
    ready = []
    for dx, bundle in enumerate(bundles):
        own_rows = o_ref.at[rows_of(n_head, dx, 0, 1, rows), :]
        ready.append(pltpu.make_async_copy(own_rows, bundle.at[0], out_sems.at[2 * dx]))
        ready.append(pltpu.make_async_copy(got_any.at[dx], bundle.at[1], out_sems.at[2 * dx + 1]))
    d = HEAD_DIM
    t, own = q_ref.shape
    tile = jnp.sum(sums_ref[...], axis=0)
    blocks = t // d
    turned = jnp.transpose(jnp.concatenate([tile] * (d // tile.shape[0]), axis=0))
    inv = lax.rsqrt(turned[:, :blocks] / width + EPS)
    fall = inv * inv * inv * (turned[:, blocks : 2 * blocks] / width)
    copies = []
    for r in range(blocks):
        at = slice(r * d, (r + 1) * d)
        a = jnp.broadcast_to(inv[:, r : r + 1], (d, d))
        b = jnp.broadcast_to(fall[:, r : r + 1], (d, d))
        for h in range(own // d):
            cols = slice(h * d, (h + 1) * d)
            do = a * w_ref[at, cols].astype(F32) - b * o_ref[at, cols].astype(F32)
            do_ref[at, cols] = do.astype(BF16)
        copies.append(
            pltpu.make_async_copy(
                do_ref.at[pl.ds(r * d, d), :], do_hbm.at[pl.ds(r * d, d), :], sems.at[r]
            )
        )
        copies[r].start()
        start_all(ready[r * len(ready) // blocks : (r + 1) * len(ready) // blocks])
    for h in range(own // d):
        cols = slice(h * d, (h + 1) * d)
        z_ref[h] = mm_at(q_ref[:, cols], do_ref[:, cols]).astype(z_ref.dtype)
    wait_all(copies + ready)


def back_kernel(first, q_hbm, k_hbm, v_hbm, do_hbm, t_hbm, p_ref, *refs):
    ak_hbm, av_hbm, gq_hbm, q_ref, k_ref, v_ref, do_ref, t_ref = refs[-13:-5]
    ak_ref, av_ref, gq_ref, sems, out_sems = refs[-5:]
    t, own = q_ref.shape
    half = t // 2
    n = own // (2 * HEAD_DIM)
    q_hbm, k_hbm, v_hbm, do_hbm, gq_hbm = [
        x.at[:, pl.ds(first * HEAD_DIM, own)] for x in (q_hbm, k_hbm, v_hbm, do_hbm, gq_hbm)
    ]
    ins = [
        by_pairs(src, dst, sems, n * j)
        for j, (src, dst) in enumerate(
            ((do_hbm, do_ref), (v_hbm, v_ref), (k_hbm, k_ref), (q_hbm, q_ref))
        )
    ]
    ins.append(
        [
            pltpu.make_async_copy(
                t_hbm.at[pl.ds(2 * i, 2)], t_ref.at[pl.ds(2 * i, 2)], sems.at[4 * n + i]
            )
            for i in range(n)
        ]
    )
    for i in range(n):
        for c in ins:
            c[i].start()
    outs = [
        by_pairs(src, dst, out_sems, n * j)
        for j, (src, dst) in enumerate(((gq_ref, gq_hbm), (ak_ref, ak_hbm), (av_ref, av_hbm)))
    ]
    low = lower(half)
    one, two = slice(0, half), slice(half, t)
    for i in range(n):
        for c in ins:
            c[i].wait()
        pair = []
        for h in range(2 * i, 2 * i + 2):
            cols = slice(h * HEAD_DIM, (h + 1) * HEAD_DIM)
            v, do = v_ref[:, cols], do_ref[:, cols]
            g0 = jnp.where(low, mm_bt(do[one], v[one]), 0.0).astype(BF16)
            g2 = mm_bt(do[two], v[one]).astype(BF16)
            g1 = jnp.where(low, mm_bt(do[two], v[two]), 0.0).astype(BF16)
            pair.append((h, cols, g0, g1, g2))
        for h, cols, _, _, _ in pair:
            dot = do_ref[:, cols].T
            s0, s1, s2 = t_ref[h, 0], t_ref[h, 1], t_ref[h, 2]
            av = mm(dot, jnp.concatenate([s0, s2], axis=0))
            av_ref[one, cols] = av.astype(BF16).T
            av_ref[two, cols] = mm(dot[:, two], s1).astype(BF16).T
        for h, cols, g0, g1, g2 in pair:
            qt, kt, dot = q_ref[:, cols].T, k_ref[:, cols].T, do_ref[:, cols].T
            base = mm(p_ref[first + h], dot)
            gq_ref[one, cols] = (mm_bt(kt[:, one], g0) + base[:, one]).astype(BF16).T
            gq = mm_bt(kt, jnp.concatenate([g2, g1], axis=1)) + base[:, two]
            gq_ref[two, cols] = gq.astype(BF16).T
            ak = mm(qt, jnp.concatenate([g0, g2], axis=0))
            ak_ref[one, cols] = ak.astype(BF16).T
            ak_ref[two, cols] = mm(qt[:, two], g1).astype(BF16).T
        for c in outs:
            c[i].start()
    for c in outs:
        wait_all(c)


def last_kernel(
    ak0_hbm, ak1_hbm, av0_hbm, av1_hbm, k_ref, v_ref, s_ref, gk_hbm, gv_hbm,
    ak_ref, av_ref, gk_ref, gv_ref, sems, out_sems,
):
    d = HEAD_DIM
    t, own = k_ref.shape
    n = own // (2 * d)
    ins = []
    for j, (dst, srcs) in enumerate(((av_ref, (av0_hbm, av1_hbm)), (ak_ref, (ak0_hbm, ak1_hbm)))):
        parts_of = []
        for m, src in enumerate(srcs):
            part = dst.at[:, pl.ds(m * own // 2, own // 2)]
            parts_of += by_pairs(src, part, sems, n * j + m * n // 2)
        ins.append(parts_of)
    for i in range(n):
        for c in ins:
            c[i].start()
    ck, cv = by_pairs(gk_ref, gk_hbm, out_sems, 0), by_pairs(gv_ref, gv_hbm, out_sems, n)
    for i in range(n):
        for c in ins:
            c[i].wait()
        for h in range(2 * i, 2 * i + 2):
            cols = slice(h * d, (h + 1) * d)
            for r in range(0, t, 256):
                rows = slice(r, r + 256)
                gv = av_ref[rows, cols].astype(F32) + mm(k_ref[rows, cols], s_ref[h])
                gv_ref[rows, cols] = gv.astype(BF16)
                gk = ak_ref[rows, cols].astype(F32) + mm_bt(v_ref[rows, cols], s_ref[h])
                gk_ref[rows, cols] = gk.astype(BF16)
        cv[i].start()
        ck[i].start()
    wait_all(ck + cv)


def gate_kernel(n, *refs):
    chips = n // 2
    srcs, gain_ref, gg_hbm = refs[: chips + 2], refs[chips + 2], refs[chips + 3]
    dsts, (gg_ref, sems, out_sems) = refs[chips + 4 : 2 * chips + 6], refs[2 * chips + 6 :]
    loads = start_all(
        [pltpu.make_async_copy(x, y, sems.at[j]) for j, (x, y) in enumerate(zip(srcs, dsts))]
    )
    *o_refs, gate_ref, grad_ref = dsts
    wide = o_refs[0].shape[2]
    total = None
    for dx in range(chips):
        loads[dx].wait()
        for dc in range(2):
            o = o_refs[dx][dc].astype(F32)
            o = jnp.sum(o * o, axis=1, keepdims=True)
            total = o if total is None else total + o
    inv = lax.rsqrt(total / (n * wide) + EPS)
    wait_all(loads[chips:])
    stores = []
    for dx in range(chips):
        for dc in range(2):
            cols = pl.ds(pl.multiple_of(place(n, dx, dc, -1) * wide, wide), wide)
            g = gate_ref[:, cols].astype(F32)
            s = jax.nn.sigmoid(g)
            scaled = grad_ref[:, cols].astype(F32) * gain_ref[:, cols]
            normed = o_refs[dx][dc].astype(F32) * inv
            gg_ref[:, cols] = (scaled * normed * s * (1.0 + g * (1.0 - s))).astype(BF16)
            store = pltpu.make_async_copy(
                gg_ref.at[:, cols], gg_hbm.at[:, cols], out_sems.at[2 * dx + dc]
            )
            store.start()
            stores.append(store)
    wait_all(stores)


def on_device(query, key_in, value, gate, gain, grad_out):
    d = HEAD_DIM
    t, own = query.shape
    heads = own // d
    rows, width = gate.shape
    n_seq, n_head = lax.axis_size("seq"), lax.axis_size("head")
    pairs, chips = heads // 2, n_head // 2
    gain = gain.reshape(1, width)

    def sds(shape, dtype):
        return jax.ShapeDtypeStruct(shape, dtype)

    def dma(n):
        return pltpu.SemaphoreType.DMA((n,))

    anywhere = pl.BlockSpec(memory_space=pl.ANY)
    whole = pl.BlockSpec(memory_space=pltpu.VMEM)
    small = 2 * t * d * d * heads
    large = 2 * t * t * d * heads
    full = pltpu.VMEM((t, own), BF16)
    full32 = pltpu.VMEM((t, own), F32)
    piece = (n_seq, heads * d // n_seq, d)

    def exchange(states):
        return lax.all_to_all(states.reshape(piece), "seq", 0, 0, tiled=True)

    def running(states, reverse, *after):
        return pl.pallas_call(
            functools.partial(running_kernel, reverse),
            out_shape=pltpu.HBM(piece, BF16),
            in_specs=[whole] + [anywhere] * len(after),
            out_specs=whole,
            compiler_params=params(),
            cost_estimate=cost(heads * d * d, 4 * heads * d * d),
            name="running",
        )(states, *after)

    keys, values = in_vmem(key_in), in_vmem(value)
    query, key_in, value = in_hbm(query), in_hbm(key_in), in_hbm(value)
    states = pl.pallas_call(
        state_kernel,
        out_shape=sds((heads, d, d), BF16),
        in_specs=[anywhere, anywhere],
        out_specs=whole,
        scratch_shapes=[full, full, dma(2 * pairs)],
        compiler_params=params(),
        cost_estimate=cost(2 * small, 4 * t * own),
        name="states",
    )(key_in, value)
    received = exchange(states)

    bundle = (2, rows, own)
    weighted = pl.pallas_call(
        functools.partial(weigh_kernel, n_head),
        out_shape=[sds(bundle, BF16)] * chips,
        compiler_params=params(),
        cost_estimate=cost(20 * rows * width, 6 * rows * width),
        name="weigh",
    )(gate, grad_out, gain)
    own_bundle = weighted[0]
    weighted = [in_hbm(w) for w in send_all(weighted)]

    tiles = (heads, 3, t // 2, t // 2)
    some = heads // 2
    tiles = (some, 3, t // 2, t // 2)

    def intra(first, *after):
        part = pltpu.VMEM((t, own // 2), BF16)
        inner, scores = pl.pallas_call(
            functools.partial(intra_kernel, first),
            out_shape=[pltpu.HBM((t, own // 2), F32), pltpu.HBM(tiles, BF16)],
            in_specs=[anywhere] * (3 + len(after)),
            out_specs=[anywhere, anywhere],
            scratch_shapes=[part] * 3
            + [pltpu.VMEM((t, own // 2), F32), pltpu.VMEM(tiles, BF16), dma(3 * some), dma(2 * some)],
            compiler_params=params(),
            cost_estimate=cost(large, 8 * t * own),
            name="intra",
        )(query, key_in, value, *after)
        return in_hbm(inner), in_hbm(scores)

    inner0, scores0 = intra(0, states)
    summed = running(received, False, own_bundle, inner0)
    prefix = exchange(summed).reshape(heads, d, d)
    inner1, scores1 = intra(some, in_hbm(summed), *weighted[1:chips])

    tile = (n_head, 2 * t // d, d)
    sums, out, weighted, queries, given = pl.pallas_call(
        functools.partial(out_kernel, n_head),
        out_shape=[sds(tile, F32), full, full, full, pltpu.HBM((chips, rows, own), BF16)],
        in_specs=[anywhere] * 3 + [whole] + [anywhere] * n_head,
        out_specs=[whole] * 4 + [anywhere],
        scratch_shapes=[full32, dma(3 * t // d + n_head), dma(chips)],
        compiler_params=params(),
        cost_estimate=cost(small, 10 * t * own),
        name="outs",
    )(inner0, inner1, query, prefix, *weighted)
    sums = lax.all_to_all(sums, "head", 0, 0, tiled=True)

    got = lax.ppermute(given, "head", [(i, i ^ 1) for i in range(n_head)])
    states, grad_attn, *bundles = pl.pallas_call(
        functools.partial(grad_kernel, n_head, float(width)),
        out_shape=[sds((heads, d, d), BF16), pltpu.HBM((t, own), BF16)]
        + [pltpu.HBM(bundle, BF16)] * chips,
        in_specs=[whole] * 4 + [anywhere],
        out_specs=[whole] + [anywhere] * (1 + chips),
        scratch_shapes=[full, dma(t // d), dma(n_head)],
        compiler_params=params(),
        cost_estimate=cost(small, 8 * t * own),
        name="grads",
    )(sums, in_vmem(queries), in_vmem(weighted), in_vmem(out), got)
    received = exchange(states)

    grad_attn = in_hbm(grad_attn)

    def back(first, scores, into, *after):
        part = pltpu.VMEM((t, own // 2), BF16)
        return pl.pallas_call(
            functools.partial(back_kernel, first),
            out_shape=[pltpu.HBM((t, own // 2), BF16)] * 2 + [sds((t, own), BF16)],
            in_specs=[anywhere] * 5 + [whole] + [anywhere] * (len(into) + len(after)),
            out_specs=[anywhere] * 3,
            scratch_shapes=[part] * 4 + [pltpu.VMEM(tiles, BF16)] + [part] * 3
            + [dma(5 * pairs // 2), dma(3 * pairs // 2)],
            input_output_aliases={6: 2} if into else {},
            compiler_params=params(),
            cost_estimate=cost(2 * large, 10 * t * own),
            name="backs",
        )(query, key_in, value, grad_attn, scores, prefix, *into, *after)

    key0, value0, grad_query = back(0, scores0, [])
    key0, value0 = in_hbm(key0), in_hbm(value0)
    summed = running(received, True, key0)
    suffix = exchange(summed).reshape(heads, d, d)
    key1, value1, grad_query = back(some, scores1, [grad_query], in_hbm(summed))
    key1, value1 = in_hbm(key1), in_hbm(value1)

    token_rows = across(bundles)
    strip = pltpu.VMEM((rows, width), BF16)
    grad_gate = pl.pallas_call(
        functools.partial(gate_kernel, n_head),
        out_shape=sds((rows, width), BF16),
        in_specs=[anywhere] * (chips + 2) + [whole],
        out_specs=anywhere,
        scratch_shapes=[pltpu.VMEM(bundle, BF16)] * chips
        + [strip, strip, strip, dma(chips + 2), dma(n_head)],
        compiler_params=params(),
        cost_estimate=cost(30 * large, 200 * t * own),
        name="gates",
    )(in_hbm(token_rows[0]), *token_rows[1:], in_hbm(gate), in_hbm(grad_out), gain)

    grad_key, grad_value = pl.pallas_call(
        last_kernel,
        out_shape=[sds((t, own), BF16), sds((t, own), BF16)],
        in_specs=[anywhere] * 4 + [whole] * 3,
        out_specs=[anywhere] * 2,
        scratch_shapes=[full] * 4 + [dma(2 * pairs), dma(2 * pairs)],
        compiler_params=params(),
        cost_estimate=cost(2 * small, 16 * t * own),
        name="last",
    )(key0, key1, value0, value1, keys, values, suffix)
    return grad_query, grad_key, grad_value, grad_gate


def solution(mesh):
    in_specs = (
        P("seq", "head"),
        P("seq", "head"),
        P("seq", "head"),
        P(("seq", "head"), None),
        P(),
        P(("seq", "head"), None),
    )
    out_specs = (P("seq", "head"), P("seq", "head"), P("seq", "head"), P(("seq", "head"), None))
    return jax.shard_map(
        on_device, mesh=mesh, in_specs=in_specs, out_specs=out_specs, check_vma=False
    )
```
